32 devices in a mesh: row: 8 (over z, x), blk: 4 (over y, core).
Axes of the slice: x: 2, y: 2, z: 4, core: 2. Of those that a mesh axis runs over, the one named last changes fastest.
Arguments:
- source_table: bfloat16 [2048, 512], P('blk'), may hold values from -6 to 6
- target_table: bfloat16 [16384, 512], P(('row', 'blk')), may hold values from -6 to 6
- message_weight: bfloat16 [512, 512], replicated, may hold values from -0.25 to 0.25
- self_weight: bfloat16 [512, 512], replicated, may hold values from -0.25 to 0.25
- tile_lists: int32 [32, 4], P(('row', 'blk')), may hold values from 0 to 3, each once within a row
- key_offsets: int32 [16384, 4], P(('row', 'blk')), may hold values from 0 to 511
- list_lengths: int32 [32], P(('row', 'blk')), may hold values from 1 to 4, 64 in all
- cotangent: bfloat16 [16384, 512], P(('row', 'blk')), may hold values from -6 to 6
Outputs:
- updated: bfloat16 [16384, 512], P(('row', 'blk'))
- target_gradient: bfloat16 [16384, 512], P(('row', 'blk'))
- source_gradient: bfloat16 [2048, 512], P(('blk', 'row'))
- self_gradient: float32 [512, 512], replicated
- message_gradient: float32 [512, 512], replicated
The draws below stay inside these ranges and needn't reach their ends.
Inputs may be any that keep to these rules, and one draw needn't show every extreme that they name: Each row of tile_lists names every one of the 4 source tiles once. A target tile uses the first list_lengths entries of its row of tile_lists.
All inputs are finite; a program needn't handle non-finite values. No bound on the sum of `list_lengths` on one device may be relied on, other than what follows from the above.
Results may differ from the reference program's by a relative error of at most 0.0058.
Values may be sent and summed in bfloat16 or wider, within the bound.
No kernel may reach another device: no remote copies, remote signals or barrier semaphores. Data moves between devices by JAX's collectives and lax.ppermute only.
A program may use at most 64 MiB of HBM per device.

```python
import math
import jax
import jax.numpy as jnp
import numpy as np
from jax import lax

HIDDEN_SIZE = 512
TILE = 512
TARGET_TILES = 32
SOURCE_TILES = 4
TARGET_ROWS = 16384
SOURCE_ROWS = 2048


def touch_ends(entries, key, smallest, top_value):
    place = [jax.random.randint(jax.random.fold_in(key, axis), (), 0, length) for axis, length in enumerate(entries.shape)]
    widest = entries.shape.index(max(entries.shape))
    neighbour = place[:widest] + [(place[widest] + 1) % entries.shape[widest]] + place[widest + 1:]
    return entries.at[tuple(place)].set(smallest).at[tuple(neighbour)].set(top_value)


def levels(stream_key, dims, pieces, least, top_value):
    loudness = 1.0
    for axis_at, shards_of in pieces:
        heights = jax.random.uniform(jax.random.fold_in(jax.random.fold_in(stream_key, 6), axis_at), (shards_of,), jnp.float32, least / len(pieces), top_value / len(pieces))
        loudness = loudness * jnp.repeat(jnp.exp(heights), dims[axis_at] // shards_of).reshape((-1,) + (1,) * (len(dims) - 1 - axis_at))
    return loudness


def split_up(count, total, most, skew):
    portions = [(1 << 20) // math.isqrt(rank ** skew) + 1 for rank in range(2, count + 1)]
    rest, holding = total - most - (count - 1), [1] * (count - 1)
    while rest > 0:
        free = [i for i in range(count - 1) if holding[i] < most]
        pool, left = sum([portions[i] for i in free]), rest
        for i in free:
            addition = min(most - holding[i], max(1, left * portions[i] // pool), rest)
            holding[i] = holding[i] + addition
            rest = rest - addition
    return np.array([most] + holding)


def ragged_sizes(key, amount, total, most, skew):
    if amount == 2:
        one = jax.random.randint(key, (), max(1, total - most), min(most, total - 1) + 1)
        return jnp.stack([one, total - one])
    lengths = jnp.asarray(split_up(amount, total, most, skew), jnp.int32)
    twos = (amount - 1) // 2
    giver, sink = lengths[1:1 + 2 * twos:2], lengths[2:2 + 2 * twos:2]
    room = jnp.minimum(giver - 1, most - sink)
    moved = jax.random.randint(jax.random.fold_in(key, 1), (twos,), 0, 1 << 20) % (room + 1)
    lengths = lengths.at[1:1 + 2 * twos:2].set(giver - moved).at[2:2 + 2 * twos:2].set(sink + moved)
    return lengths[jax.random.permutation(jax.random.fold_in(key, 2), amount)]


def noise(key, extent, scale, most, cuts=(), kind=jnp.bfloat16):
    array = scale * jax.random.normal(key, extent, jnp.float32)
    if cuts:
        array = array * levels(key, extent, cuts, -0.22, 0.18)
    return jnp.clip(array, -most, most).astype(kind)


def setup_inputs(seed: int = 0) -> dict:
    seeds = jax.random.split(jax.random.key(seed), 9)
    return {
        "source_table": noise(seeds[0], (SOURCE_ROWS, HIDDEN_SIZE), 1.0, 6.0, ((0, 4),)),
        "target_table": noise(seeds[1], (TARGET_ROWS, HIDDEN_SIZE), 1.0, 6.0, ((0, 32),)),
        "message_weight": noise(seeds[2], (HIDDEN_SIZE, HIDDEN_SIZE), HIDDEN_SIZE ** -0.5, 0.25),
        "self_weight": noise(seeds[3], (HIDDEN_SIZE, HIDDEN_SIZE), HIDDEN_SIZE ** -0.5, 0.25),
        "tile_lists": jax.vmap(lambda own: jax.random.permutation(own, SOURCE_TILES))(jax.random.split(seeds[4], TARGET_TILES)).reshape((TARGET_TILES, SOURCE_TILES)).astype(jnp.int32),
        "key_offsets": touch_ends(jax.random.randint(seeds[5], (TARGET_ROWS, SOURCE_TILES), 0, TILE), jax.random.fold_in(seeds[5], 1), 0, TILE - 1).astype(jnp.int32),
        "list_lengths": ragged_sizes(seeds[6], TARGET_TILES, TARGET_TILES * SOURCE_TILES // 2, SOURCE_TILES, 2).astype(jnp.int32),
        "cotangent": noise(seeds[7], (TARGET_ROWS, HIDDEN_SIZE), 1.0, 6.0, ((0, 32),)),
    }


def reference(source_table, target_table, message_weight, self_weight, tile_lists, key_offsets, list_lengths, cotangent):
    projected = jnp.dot(source_table, message_weight, preferred_element_type=jnp.float32).astype(jnp.bfloat16)
    row_tile = (jnp.arange(TARGET_ROWS) // TILE).astype(jnp.int32)
    row_length = list_lengths[row_tile]
    inverse = 1.0 / row_length.astype(jnp.float32)
    linked = (tile_lists[row_tile] * TILE + key_offsets).astype(jnp.int32)
    active = jnp.arange(SOURCE_TILES, dtype=jnp.int32)[None, :] < row_length[:, None]

    def gather_step(totals, inputs):
        index_col, active_col = inputs
        values = projected[index_col].astype(jnp.float32)
        return totals + jnp.where(active_col[:, None], values, jnp.float32(0.0)), None

    start_sum = jnp.zeros((TARGET_ROWS, HIDDEN_SIZE), jnp.float32)
    gathered, _ = lax.scan(gather_step, start_sum, (linked.T, active.T))
    gathered = gathered * inverse[:, None]
    preact = jnp.dot(target_table, self_weight, preferred_element_type=jnp.float32) + gathered
    sigmoid_pre = jax.nn.sigmoid(preact)
    updated = (target_table.astype(jnp.float32) + preact * sigmoid_pre).astype(jnp.bfloat16)
    upstream = cotangent.astype(jnp.float32)
    grad_pre = (upstream * sigmoid_pre * (1.0 + preact * (1.0 - sigmoid_pre))).astype(jnp.bfloat16)
    target_gradient = (upstream + jnp.dot(grad_pre, self_weight.T, preferred_element_type=jnp.float32)).astype(jnp.bfloat16)
    self_gradient = jnp.dot(target_table.T, grad_pre, preferred_element_type=jnp.float32) * (TARGET_ROWS ** -0.5)
    scaled = grad_pre.astype(jnp.float32) * inverse[:, None]

    def scatter_step(totals, inputs):
        index_col, active_col = inputs
        terms = jnp.where(active_col[:, None], scaled, jnp.float32(0.0))
        return totals + jax.ops.segment_sum(terms, index_col, num_segments=SOURCE_ROWS), None

    start_grad = jnp.zeros((SOURCE_ROWS, HIDDEN_SIZE), jnp.float32)
    source_sum, _ = lax.scan(scatter_step, start_grad, (linked.T, active.T))
    source_grad_rounded = source_sum.astype(jnp.bfloat16)
    source_gradient = jnp.dot(source_grad_rounded, message_weight.T, preferred_element_type=jnp.float32).astype(jnp.bfloat16)
    message_gradient = jnp.dot(source_table.T, source_grad_rounded, preferred_element_type=jnp.float32) * (SOURCE_ROWS ** -0.5)
    return updated, target_gradient, source_gradient, self_gradient, message_gradient
```

```python
import functools

import jax
import jax.numpy as jnp
from jax import lax
from jax.experimental import pallas as pl
from jax.experimental.pallas import tpu as pltpu
from jax.sharding import PartitionSpec as P

AXES = ("row", "blk")
BF16 = jnp.bfloat16
F32 = jnp.float32
SMEM = pl.BlockSpec(memory_space=pltpu.SMEM)
VMEM = pl.BlockSpec(memory_space=pltpu.VMEM)
VMEM_BYTES = 48 * 1024 * 1024


def swap(value, mask, devices):
    return lax.ppermute(value, AXES, [(i, i ^ mask) for i in range(devices)])


def call(body, name, out_shape, scratch=(), flops=0, moved=0):
    return pl.pallas_call(
        body,
        name=name,
        out_shape=out_shape,
        scratch_shapes=scratch,
        compiler_params=pltpu.CompilerParams(vmem_limit_bytes=VMEM_BYTES),
        cost_estimate=pl.CostEstimate(flops=flops, bytes_accessed=moved, transcendentals=0),
    )


def shaped(shape, dtype):
    return jax.ShapeDtypeStruct(shape, dtype)


def mm(a, b, dims=((1,), (0,))):
    return lax.dot_general(a, b, (dims, ((), ())), preferred_element_type=F32)


def gather_first(links_ref, s0_ref, s1_ref, t_ref, ws_ref, own_ref, h_ref):
    own_ref[...] = mm(t_ref[...], ws_ref[...])
    links = links_ref[...].T
    rows = t_ref.shape[0]
    lanes = lax.broadcasted_iota(jnp.int32, (rows, rows), 1)
    total = None
    for m, s_ref in enumerate((s0_ref, s1_ref)):
        pattern = (links[:, m : m + 1] == lanes).astype(F32).astype(BF16)
        added = mm(pattern, s_ref[...])
        total = added if total is None else total + added
    h_ref[...] = total


def gather_rest(links_ref, h0_ref, *refs):
    s_refs, hb_ref = refs[:-1], refs[-1]
    links = links_ref[...].T
    rows = h0_ref.shape[0]
    lanes = lax.broadcasted_iota(jnp.int32, (rows, rows), 1)
    total = h0_ref[...]
    for m, s_ref in enumerate(s_refs):
        pattern = (links[:, m + 2 : m + 3] == lanes).astype(F32).astype(BF16)
        total = total + mm(pattern, s_ref[...])
    hb_ref[...] = total.astype(BF16)


def activate(length_ref, hb_ref, own_ref, wm_ref, t_ref, cot_ref, updated_ref, grad_ref):
    inverse = 1.0 / jnp.full((1, hb_ref.shape[1]), length_ref[0], jnp.int32).astype(F32)
    preact = own_ref[...] + mm(hb_ref[...], wm_ref[...]) * inverse
    sig = jax.nn.sigmoid(preact)
    updated_ref[...] = (t_ref[...].astype(F32) + preact * sig).astype(BF16)
    grad_ref[...] = (cot_ref[...].astype(F32) * sig * (1.0 + preact * (1.0 - sig))).astype(BF16)


def weight_terms(place_ref, lengths_ref, x0_ref, x1_ref, g0_ref, g1_ref, *refs):
    own_ref, sent_refs, total_ref = refs[0], refs[1:-1], refs[-1]
    core = place_ref[0]
    quad = place_ref[1]
    rows = own_ref.shape[0]
    width = own_ref.shape[1]

    def factor(i):
        length = jnp.where(core == 0, 1, lengths_ref[i])
        return 1.0 / jnp.full((1, width), length, jnp.int32).astype(F32)

    dims = ((0,), (0,))
    total_ref[...] = mm(x0_ref[...], g0_ref[...], dims) * factor(0) + mm(x1_ref[...], g1_ref[...], dims) * factor(1)
    own_ref[...] = total_ref[pl.ds(pl.multiple_of(quad * rows, rows), rows), :]
    for m, ref in enumerate(sent_refs, 1):
        ref[...] = total_ref[pl.ds(pl.multiple_of((quad ^ m) * rows, rows), rows), :].astype(BF16)


def source_terms(share, sides, place_ref, lengths_ref, l0_ref, l1_ref, g0_ref, g1_ref, *refs):
    core = place_ref[0]
    quad = place_ref[1]
    rows, width = refs[0].shape
    targets = g0_ref.shape[0]
    position = lax.broadcasted_iota(jnp.int32, (rows, targets), 0)
    inside = (position // share) * (2 * share) + position % share
    inverses = [1.0 / jnp.full((1, width), lengths_ref[i], jnp.int32).astype(F32) for i in range(2)]
    for m, ref in enumerate(refs):
        to = quad ^ m
        block = (to % sides) * 2 + core
        row_at = inside + (to // sides) * share
        total = None
        for i, (l_ref, g_ref) in enumerate(((l0_ref, g0_ref), (l1_ref, g1_ref))):
            pattern = (l_ref[pl.ds(block, 1), :] == row_at).astype(F32).astype(BF16)
            added = mm(pattern, g_ref[...]) * inverses[i]
            total = added if total is None else total + added
        ref[...] = total.astype(ref.dtype)


def add_up(own_ref, *refs):
    out_ref = refs[-1]
    total = own_ref[...]
    for ref in refs[:-1]:
        total = total + ref[...].astype(F32)
    out_ref[...] = total.astype(BF16)


def add_tree(*refs):
    values = [ref[...].astype(F32) for ref in refs[:-1]]
    while len(values) > 1:
        values = [values[i] + values[i + 1] for i in range(0, len(values), 2)]
    refs[-1][...] = values[0].astype(BF16)


def split_sum(peers, place_ref, own_ref, *refs):
    received, outs, total_ref = refs[:peers], refs[peers:-1], refs[-1]
    layer = place_ref[2]
    rows = outs[0].shape[0]
    total = own_ref[...]
    for ref in received:
        total = total + ref[...].astype(F32)
    total_ref[...] = total
    for m, ref in enumerate(outs):
        at = pl.multiple_of((layer ^ m) * rows, rows)
        ref[...] = total_ref[pl.ds(at, rows), :].astype(ref.dtype)


def finish_source(wm_ref, own_ref, *refs):
    total = own_ref[...]
    for ref in refs[:-1]:
        total = total + ref[...].astype(F32)
    refs[-1][...] = mm(total.astype(BF16), wm_ref[...], ((1,), (1,))).astype(BF16)


def finish_weights(quads, scales, place_ref, *refs):
    mine, theirs, outs = refs[:quads], refs[quads : 2 * quads], refs[2 * quads :]
    core = place_ref[0]
    quad = place_ref[1]
    rows = mine[0].shape[0]

    def write(out_ref, pieces, scale):
        for m, ref in enumerate(pieces):
            at = pl.multiple_of((quad ^ m) * rows, rows)
            out_ref[pl.ds(at, rows), :] = ref[...].astype(F32) * scale

    @pl.when(core == 0)
    def _():
        write(outs[0], mine, scales[0])
        write(outs[1], theirs, scales[1])

    @pl.when(core != 0)
    def _():
        write(outs[0], theirs, scales[0])
        write(outs[1], mine, scales[1])


def local(row_devices, blk_devices, source_table, target_table, message_weight, self_weight, tile_lists, key_offsets, list_lengths, cotangent):
    devices = row_devices * blk_devices
    targets, width = target_table.shape
    block_rows = source_table.shape[0]
    slots = tile_lists.shape[1]
    assert tile_lists.shape[0] == 1 and block_rows == targets and slots == blk_devices
    sides = blk_devices // 2
    quads = blk_devices
    layers = row_devices // 2
    share = block_rows // row_devices

    row_at = lax.axis_index("row")
    blk_at = lax.axis_index("blk")
    core = blk_at % 2
    quad = (row_at % 2) * sides + blk_at // 2
    layer = row_at // 2
    place = jnp.stack([core, quad, layer]).astype(jnp.int32)

    blocks = lax.iota(jnp.int32, blk_devices)
    used = (tile_lists[0][None, :] == blocks[:, None]) & (lax.iota(jnp.int32, slots)[None, :] < list_lengths[0])
    links = jnp.max(jnp.where(used[:, :, None], key_offsets.T[None, :, :], -1), axis=1)
    near = jnp.max(jnp.where((blocks[:, None] ^ blk_at) == blocks[None, :], 1, 0)[:, :, None] * (links[None, :, :] + 1), axis=1) - 1
    near = jnp.pad(near, ((0, -slots % 8), (0, 0)), constant_values=-1)
    links = jnp.pad(links, ((0, -slots % 8), (0, 0)), constant_values=-1)

    held = {0: source_table, 1: swap(source_table, 1, devices)}
    for m in range(2, blk_devices, 2):
        held[m] = swap(source_table, m, devices)
        held[m + 1] = swap(held[m], 1, devices)
    packed = jnp.concatenate([links, jnp.broadcast_to(list_lengths[:, None], (8, targets))], axis=0)
    packed = swap(packed, 1, devices)
    their_links = packed[: links.shape[0]]
    lengths = jnp.stack([list_lengths[0], packed[links.shape[0], 0]])

    square = 2 * targets * width * width
    own_term, gathered = call(
        gather_first, "gather_first", (shaped((targets, width), F32),) * 2, flops=3 * square, moved=5 << 20
    )(near, held[0], held[1], target_table, self_weight)
    gathered = call(gather_rest, "gather_rest", shaped((targets, width), BF16), flops=2 * square, moved=3 << 20)(
        near, gathered, *[held[m] for m in range(2, blk_devices)]
    )
    mine = jnp.where(core == 0, target_table, gathered)
    other = jnp.where(core == 0, gathered, target_table)
    other = swap(other, 1, devices)
    updated, grad_pre = pl.pallas_call(
        activate,
        name="activate",
        in_specs=[SMEM] + [VMEM] * 5,
        out_shape=(shaped((targets, width), BF16),) * 2,
        compiler_params=pltpu.CompilerParams(vmem_limit_bytes=VMEM_BYTES),
        cost_estimate=pl.CostEstimate(flops=square, bytes_accessed=4 << 20, transcendentals=targets * width),
    )(list_lengths, gathered, own_term, message_weight, target_table, cotangent)
    their_grad = swap(grad_pre, 1, devices)

    piece = width // quads
    terms = pl.pallas_call(
        weight_terms,
        name="weight_terms",
        in_specs=[SMEM] * 2 + [VMEM] * 4,
        out_shape=[shaped((piece, width), F32)] + [shaped((piece, width), BF16)] * (quads - 1),
        scratch_shapes=[pltpu.VMEM((width, width), F32)],
        compiler_params=pltpu.CompilerParams(vmem_limit_bytes=VMEM_BYTES),
        cost_estimate=pl.CostEstimate(flops=2 * square, bytes_accessed=3 << 20, transcendentals=0),
    )(place, lengths, mine, other, grad_pre, their_grad)
    received = [swap(terms[m], 2 * m, devices) for m in range(1, quads)]
    part = call(add_up, "weight_sum_square", shaped((piece, width), BF16), moved=1 << 20)(terms[0], *received)

    rows_out = layers * share
    sources = pl.pallas_call(
        functools.partial(source_terms, share, sides),
        name="source_terms",
        in_specs=[SMEM] * 2 + [VMEM] * 4,
        out_shape=[shaped((rows_out, width), F32)] + [shaped((rows_out, width), BF16)] * (quads - 1),
        compiler_params=pltpu.CompilerParams(vmem_limit_bytes=VMEM_BYTES),
        cost_estimate=pl.CostEstimate(flops=4 * square, bytes_accessed=3 << 20, transcendentals=0),
    )(place, lengths, links, their_links, grad_pre, their_grad)
    source_received = [swap(sources[m], 2 * m, devices) for m in range(1, quads)]

    layer_parts = [part] + [swap(part, 2 * quads * m, devices) for m in range(1, layers)]
    total = call(add_tree, "weight_sum_layers", shaped((piece, width), BF16), moved=1 << 20)(*layer_parts)

    source_parts = pl.pallas_call(
        functools.partial(split_sum, quads - 1),
        name="source_sum_square",
        in_specs=[SMEM] + [VMEM] * quads,
        out_shape=[shaped((share, width), F32)] + [shaped((share, width), BF16)] * (layers - 1),
        scratch_shapes=[pltpu.VMEM((rows_out, width), F32)],
        compiler_params=pltpu.CompilerParams(vmem_limit_bytes=VMEM_BYTES),
        cost_estimate=pl.CostEstimate(flops=0, bytes_accessed=2 << 20, transcendentals=0),
    )(place, sources[0], *source_received)
    source_last = [swap(source_parts[m], 2 * quads * m, devices) for m in range(1, layers)]
    source_gradient = call(finish_source, "finish_source", shaped((share, width), BF16), moved=1 << 20)(
        message_weight, source_parts[0], *source_last
    )

    pieces = [total] + [swap(total, 2 * m, devices) for m in range(1, quads)]
    their_pieces = [swap(value, 1, devices) for value in pieces]
    target_total = targets * devices
    source_total = block_rows * blk_devices
    self_gradient, message_gradient = pl.pallas_call(
        functools.partial(finish_weights, quads, (target_total ** (-0.5), source_total ** (-0.5))),
        name="finish_weights",
        in_specs=[SMEM] + [VMEM] * (2 * quads),
        out_shape=(shaped((width, width), F32),) * 2,
        compiler_params=pltpu.CompilerParams(vmem_limit_bytes=VMEM_BYTES),
        cost_estimate=pl.CostEstimate(flops=0, bytes_accessed=3 << 20, transcendentals=0),
    )(place, *pieces, *their_pieces)

    target_gradient = (
        cotangent.astype(F32) + jnp.dot(grad_pre, self_weight.T, preferred_element_type=F32)
    ).astype(BF16)
    return (updated, target_gradient, source_gradient, self_gradient, message_gradient)


def solution(mesh):
    split = P(AXES, None)
    return jax.shard_map(
        functools.partial(local, mesh.shape["row"], mesh.shape["blk"]),
        mesh=mesh,
        in_specs=(P("blk", None), split, P(), P(), split, split, P(AXES), split),
        out_specs=(split, split, P(("blk", "row"), None), P(), P()),
        check_vma=False,
    )
```

```python
import functools

import jax
import jax.numpy as jnp
from jax import lax
from jax.experimental import pallas as pl
from jax.experimental.pallas import tpu as pltpu
from jax.sharding import PartitionSpec as P

AXES = ("row", "blk")
BF16 = jnp.bfloat16
F32 = jnp.float32
SMEM = pl.BlockSpec(memory_space=pltpu.SMEM)
VMEM = pl.BlockSpec(memory_space=pltpu.VMEM)
HBM = pl.BlockSpec(memory_space=pltpu.HBM)
ROWS = ((0,), (0,))
LANES = ((1,), (1,))


def swap(value, mask, devices):
    return lax.ppermute(value, AXES, [(i, i ^ mask) for i in range(devices)])


def call(body, name, out_shape, scalars=0, inputs=0, flops=0, moved=1 << 20, **more):
    return pl.pallas_call(
        body,
        name=name,
        in_specs=[SMEM] * scalars + [VMEM] * inputs,
        out_shape=out_shape,
        compiler_params=pltpu.CompilerParams(vmem_limit_bytes=20 << 20),
        cost_estimate=pl.CostEstimate(flops=flops, bytes_accessed=moved, transcendentals=0),
        **more,
    )


def shaped(shape, dtype):
    return jax.ShapeDtypeStruct(shape, dtype)


def mm(a, b, dims=((1,), (0,))):
    return lax.dot_general(a, b, (dims, ((), ())), preferred_element_type=F32)


def pattern(rows, lanes):
    return (rows == lanes).astype(F32).astype(BF16)


def part(ref, core):
    half = ref.shape[1] // 2
    return ref[:, pl.ds(pl.multiple_of(core * half, half), half)]


def inverse(lengths_ref, i, width):
    return 1.0 / jnp.full((1, width), lengths_ref[i], jnp.int32).astype(F32)


def linked(column, s_ref):
    lanes = lax.broadcasted_iota(jnp.int32, (column.shape[0], s_ref.shape[0]), 1)
    return mm(pattern(column, lanes), s_ref[...])


def gather_first(place_ref, links0_ref, links1_ref, s_ref, t_ref, ws_ref, columns_ref, own_ref, h_ref, weight_ref, near_ref):
    block = place_ref[3]
    rows = t_ref.shape[0]
    weight = part(ws_ref, place_ref[0])
    weight_ref[...] = weight
    own_ref[...] = mm(t_ref[...], weight)
    for i, links_ref in enumerate((links0_ref, links1_ref)):
        span = pl.ds(i * rows, rows)
        for m in range(links_ref.shape[0]):
            near_ref[m : m + 1, :] = links_ref[pl.ds(block ^ m, 1), :]
        columns = near_ref[...].T
        columns_ref[span, :] = columns
        h_ref[span, :] = linked(columns[:, 0:1], s_ref)


def gather_middle(order, place_ref, columns_ref, h0_ref, t_ref, weight_ref, *refs):
    s_refs, own_ref, h_ref = refs[:-2], refs[-2], refs[-1]
    rows = t_ref.shape[0]
    own_ref[...] = mm(t_ref[...], weight_ref[...])
    add_linked(order, columns_ref, h0_ref, s_refs, h_ref, rows)


def gather_more(order, columns_ref, h0_ref, *refs):
    add_linked(order, columns_ref, h0_ref, refs[:-1], refs[-1], h0_ref.shape[0] // 2)


def add_linked(order, columns_ref, h0_ref, s_refs, h_ref, rows):
    for i in range(2):
        span = pl.ds(i * rows, rows)
        total = h0_ref[span, :]
        for m, s_ref in zip(order, s_refs):
            total = total + linked(columns_ref[span, m : m + 1], s_ref)
        h_ref[span, :] = total


def forward(order, place_ref, lengths_ref, columns_ref, h0_ref, own0_ref, own1_ref, wm_ref, t0_ref, t1_ref, c0_ref, c1_ref, *refs):
    s_refs, (h_ref, grad_ref, updated_ref) = refs[:-3], refs[-3:]
    core = place_ref[0]
    rows, width = t0_ref.shape
    weight = part(wm_ref, core)
    for i, (t_ref, c_ref, own_ref) in enumerate(((t0_ref, c0_ref, own0_ref), (t1_ref, c1_ref, own1_ref))):
        span = pl.ds(i * rows, rows)
        total = h0_ref[span, :]
        for m, s_ref in zip(order, s_refs):
            total = total + linked(columns_ref[span, m : m + 1], s_ref)
        gathered = (total * inverse(lengths_ref, i, width)).astype(BF16)
        h_ref[span, :] = gathered
        preact = own_ref[...] + mm(gathered, weight)
        sig = jax.nn.sigmoid(preact)
        updated_ref[span, :] = (part(t_ref, core).astype(F32) + preact * sig).astype(BF16)
        upstream = part(c_ref, core).astype(F32)
        grad_ref[span, :] = (upstream * sig * (1.0 + preact * (1.0 - sig))).astype(BF16)


def weight_terms(place_ref, t0_ref, t1_ref, h_ref, grad_ref, *refs):
    own_ref, sent_refs, total_ref = refs[0], refs[1:-1], refs[-1]
    quad = place_ref[1]
    rows, width = t0_ref.shape
    piece = own_ref.shape[0]
    total_ref[0:width, :] = mm(t0_ref[...], grad_ref[0:rows, :], ROWS) + mm(t1_ref[...], grad_ref[rows:, :], ROWS)
    total_ref[width:, :] = mm(h_ref[...], grad_ref[...], ROWS)
    for m, ref in enumerate((own_ref, *sent_refs)):
        at = pl.multiple_of((quad ^ m) * piece, piece)
        ref[...] = total_ref[pl.ds(at, piece), :].astype(ref.dtype)


def source_terms(share, sides, orders, place_ref, lengths_ref, links0_ref, links1_ref, grad_ref, other_ref, *refs):
    core, quad, layer = place_ref[0], place_ref[1], place_ref[2]
    targets = links0_ref.shape[1]
    half = grad_ref.shape[1]
    rows = 2 * refs[0].shape[0] // len(orders[0])
    position = lax.broadcasted_iota(jnp.int32, (rows, targets), 0)
    inverses = [inverse(lengths_ref, i, half) for i in range(2)]
    for n, order in enumerate(orders):
        far = reverse_bits(position // share + n * (rows // share), 2 * rows // share)
        inside = (layer ^ far) * (2 * share) + position % share
        for j, m in enumerate(order):
            ref = refs[2 * n + j // (len(order) // 2)]
            at = (j % (len(order) // 2)) * rows
            to = quad ^ m
            row_at = inside + (to // sides) * share
            block = (to % sides) * 2 + core
            totals = [None, None]
            for i, links_ref in enumerate((links0_ref, links1_ref)):
                chosen = pattern(links_ref[pl.ds(block, 1), :], row_at)
                for c, g_ref in enumerate((grad_ref, other_ref)):
                    at_target = (i ^ c) * targets
                    added = mm(chosen, g_ref[at_target : at_target + targets, :]) * inverses[i]
                    totals[c] = added if totals[c] is None else totals[c] + added
            first = core == 0
            ref[at : at + rows, 0:half] = jnp.where(first, totals[0], totals[1]).astype(ref.dtype)
            ref[at : at + rows, half:] = jnp.where(first, totals[1], totals[0]).astype(ref.dtype)


def reverse_bits(value, size):
    result, low, high = value * 0, 1, size // 2
    while high:
        result = result + ((value // low) % 2) * high
        low, high = low * 2, high // 2
    return result


def halve(own_ref, received_ref, *refs):
    rows = refs[0].shape[0]
    for n, ref in enumerate(refs):
        span = pl.ds(n * rows, rows)
        ref[...] = (own_ref[span, :] + received_ref[span, :].astype(F32)).astype(ref.dtype)


def add_up(*refs):
    total = refs[0][...].astype(F32)
    for ref in refs[1:-1]:
        total = total + ref[...].astype(F32)
    refs[-1][...] = total.astype(BF16)


def finish_source(wm_ref, own_ref, received_ref, out_ref):
    total = (own_ref[...] + received_ref[...].astype(F32)).astype(BF16)
    out_ref[...] = mm(total, wm_ref[...], LANES).astype(BF16)


def target_side(place_ref, ws_ref, cot_ref, grad_ref, grad_received_ref, held_ref, held_received_ref, out_ref, updated_ref):
    core = place_ref[0]
    rows = cot_ref.shape[0]
    out_ref[...] = (
        cot_ref[...].astype(F32)
        + mm(grad_ref[0:rows, :], part(ws_ref, core), LANES)
        + mm(grad_received_ref[rows:, :], part(ws_ref, 1 - core), LANES)
    ).astype(BF16)
    half = held_ref.shape[1]
    updated_ref[:, pl.ds(pl.multiple_of(core * half, half), half)] = held_ref[0:rows, :]
    updated_ref[:, pl.ds(pl.multiple_of((1 - core) * half, half), half)] = held_received_ref[...]


def finish_weights(quads, scales, place_ref, *refs):
    refs, outs, buffer, sems = refs[: 2 * quads], refs[-4:-2], refs[-2], refs[-1]
    core, quad = place_ref[0], place_ref[1]
    count = quads // 2
    rows, half = refs[0].shape

    def copies(n):
        slot = quad ^ (n % quads)
        column = pl.multiple_of((core if n < quads else 1 - core) * half, half)
        row = pl.multiple_of((slot % count) * rows, rows)
        return slot // count, [
            pltpu.make_async_copy(buffer.at[n], out.at[pl.ds(row, rows), pl.ds(column, half)], sems.at[n]) for out in outs
        ]

    for n, ref in enumerate(refs):
        which, pair = copies(n)
        buffer[n] = ref[...].astype(F32) * jnp.where(which == 0, scales[0], scales[1])
        for k in range(2):
            pl.when(which == k)(pair[k].start)
    for n in range(2 * quads):
        which, pair = copies(n)
        for k in range(2):
            pl.when(which == k)(pair[k].wait)


def local(row_devices, blk_devices, source_table, target_table, message_weight, self_weight, tile_lists, key_offsets, list_lengths, cotangent):
    devices = row_devices * blk_devices
    targets, width = target_table.shape
    block_rows = source_table.shape[0]
    slots = tile_lists.shape[1]
    assert tile_lists.shape[0] == 1 and block_rows == targets and slots == blk_devices
    half = width // 2
    sides = blk_devices // 2
    quads = blk_devices
    layers = row_devices // 2
    share = block_rows // row_devices
    square = 2 * targets * width * width

    row_at = lax.axis_index("row")
    blk_at = lax.axis_index("blk")
    quad = (row_at % 2) * sides + blk_at // 2
    place = jnp.stack([blk_at % 2, quad, row_at // 2, blk_at]).astype(jnp.int32)

    direct = list(range(2, blk_devices, 2))
    held = {m: swap(source_table, m, devices) for m in direct}

    blocks = lax.iota(jnp.int32, blk_devices)
    used = (tile_lists[0][None, :] == blocks[:, None]) & (lax.iota(jnp.int32, slots)[None, :] < list_lengths[0])
    links = jnp.max(jnp.where(used[:, :, None], key_offsets.T[None, :, :], -1), axis=1)
    packed = jnp.concatenate([links, jnp.broadcast_to(list_lengths[:, None], (8 - slots % 8, targets))], axis=0)
    their_packed = swap(packed, 1, devices)
    lengths = jnp.stack([packed[slots, 0], their_packed[slots, 0]])
    links, their_links = packed[:slots], their_packed[:slots]

    table0, cot0 = target_table, cotangent
    held[1] = swap(source_table, 1, devices)
    table1 = swap(table0, 1, devices)
    cot1 = swap(cot0, 1, devices)

    columns, own0, gathered, weight = call(
        gather_first,
        "gather_first",
        (
            shaped((2 * targets, slots), jnp.int32),
            shaped((targets, half), F32),
            shaped((2 * targets, width), F32),
            shaped((width, half), BF16),
        ),
        scalars=1,
        inputs=5,
        moved=0,
        scratch_shapes=[pltpu.VMEM((slots, targets), jnp.int32)],
    )(place, links, their_links, source_table, table0, self_weight)
    own1, gathered = call(
        functools.partial(gather_middle, [1]),
        "gather_middle",
        (shaped((targets, half), F32), shaped((2 * targets, width), F32)),
        scalars=1,
        inputs=5,
        moved=0,
    )(place, columns, gathered, table1, weight, held[1])
    ready = lax.optimization_barrier((columns, own0, own1, gathered, lengths, place, *[held[m] for m in direct]))
    columns, own0, own1, gathered, lengths, place = ready[:6]
    for m, value in zip(direct, ready[6:]):
        held[m] = value
        held[m + 1] = swap(value, 1, devices)
    gathered = call(
        functools.partial(gather_more, direct),
        "gather_more",
        shaped((2 * targets, width), F32),
        inputs=2 + len(direct),
        flops=2 * square,
    )(columns, gathered, *[held[m] for m in direct])
    order = [m + 1 for m in direct]
    gathered, grad, updated = call(
        functools.partial(forward, order),
        "forward",
        (
            shaped((2 * targets, width), BF16),
            shaped((2 * targets, half), BF16),
            shaped((2 * targets, half), BF16),
        ),
        scalars=2,
        inputs=9 + len(order),
        flops=2 * sides * square,
    )(
        place, lengths, columns, gathered, own0, own1, message_weight, table0, table1, cot0, cot1,
        *[held[m] for m in order],
    )

    piece = 2 * width // quads
    terms = call(
        weight_terms,
        "weight_terms",
        [shaped((piece, half), F32)] + [shaped((piece, half), BF16)] * (quads - 1),
        scalars=1,
        inputs=4,
        flops=2 * square,
        scratch_shapes=[pltpu.VMEM((2 * width, half), F32)],
    )(place, table0, table1, gathered, grad)
    received = [swap(terms[m], 2 * m, devices) for m in reversed(range(1, quads))]

    grad_received = swap(grad, 1, devices)
    updated_received = swap(updated[targets:], 1, devices)
    grad_received, updated_received = lax.optimization_barrier((grad_received, updated_received))
    masks = [1 << i for i in range(quads.bit_length() - 1)]
    routes = (masks, masks[::-1])
    orders = [[sum(mask * ((j >> (len(masks) - 1 - i)) & 1) for i, mask in enumerate(route)) for j in range(quads)] for route in routes]
    half_rows = layers * share // 2
    count = quads // 2 * half_rows
    sources = call(
        functools.partial(source_terms, share, sides, orders),
        "source_terms",
        [shaped((count, width), F32), shaped((count, width), BF16)] * 2,
        scalars=2,
        inputs=4,
        flops=4 * square,
    )(place, lengths, links, their_links, grad, grad_received)
    _, received = lax.optimization_barrier((sources, received))

    state = [[sources[0], sources[1]], [sources[2], sources[3]]]

    def source_step(n):
        return [swap(state[k][1], 2 * routes[k][n], devices) for k in range(2)]

    def source_add(n, came):
        for k in range(2):
            if n == len(masks) - 1:
                outs = [shaped((half_rows, width), (F32, BF16)[k])]
            else:
                rows = state[k][0].shape[0] // 2
                outs = [shaped((rows, width), F32), shaped((rows, width), BF16)]
            state[k] = call(halve, "source_sum", outs, inputs=2)(state[k][0], came[k])

    total = call(add_up, "weight_sum", shaped((piece, half), BF16), inputs=quads)(terms[0], *received)
    mask, n = 1, 0
    while mask < layers:
        other = swap(total, 2 * quads * mask, devices)
        came = source_step(n)
        total = call(add_up, "weight_sum", shaped((piece, half), BF16), inputs=2)(total, other)
        source_add(n, came)
        mask, n = 2 * mask, n + 1
    target_gradient, updated = call(
        target_side, "target_side", (shaped((targets, width), BF16),) * 2, scalars=1, inputs=6, flops=square
    )(place, self_weight, cot0, grad, grad_received, updated, updated_received)
    total, target_gradient, updated = lax.optimization_barrier((total, target_gradient, updated))
    while n < len(masks):
        source_add(n, source_step(n))
        n += 1
    stays, goes = state[0][0], state[1][0]
    pieces = {0: total}
    for m in reversed(range(1, quads)):
        pieces[m] = swap(total, 2 * m, devices)

    mask = 1
    while mask < layers:
        came = swap(goes, 2 * quads * mask, devices)
        mask *= 2
        if mask == layers:
            source_gradient = call(finish_source, "finish_source", shaped((share, width), BF16), inputs=3)(
                message_weight, stays, came
            )
        else:
            rows = stays.shape[0] // 2
            stays, goes = call(halve, "source_sum", [shaped((rows, width), F32), shaped((rows, width), BF16)], inputs=2)(
                stays, came
            )

    their_pieces = {m: swap(value, 1, devices) for m, value in pieces.items()}
    scales = ((targets * devices) ** (-0.5), (block_rows * blk_devices) ** (-0.5))
    self_gradient, message_gradient = call(
        functools.partial(finish_weights, quads, scales),
        "finish_weights",
        (shaped((width, width), F32),) * 2,
        scalars=1,
        inputs=2 * quads,
        out_specs=(HBM, HBM),
        scratch_shapes=[pltpu.VMEM((2 * quads, piece, half), F32), pltpu.SemaphoreType.DMA((2 * quads,))],
    )(place, *[values[m] for values in (pieces, their_pieces) for m in range(quads)])
    return (updated, target_gradient, source_gradient, self_gradient, message_gradient)


def solution(mesh):
    split = P(AXES, None)
    return jax.shard_map(
        functools.partial(local, mesh.shape["row"], mesh.shape["blk"]),
        mesh=mesh,
        in_specs=(P("blk", None), split, P(), P(), split, split, P(AXES), split),
        out_specs=(split, split, P(("blk", "row"), None), P(), P()),
        check_vma=False,
    )
```

```python
import functools

import jax
import jax.numpy as jnp
from jax import lax
from jax.experimental import pallas as pl
from jax.experimental.pallas import tpu as pltpu
from jax.sharding import PartitionSpec as P

AXES = ("row", "blk")
BF16 = jnp.bfloat16
F32 = jnp.float32
VMEM = pl.BlockSpec(memory_space=pltpu.VMEM)
HBM = pl.BlockSpec(memory_space=pltpu.HBM)
ROWS = ((0,), (0,))
LANES = ((1,), (1,))


def swap(value, mask, devices):
    return lax.ppermute(value, AXES, [(i, i ^ mask) for i in range(devices)])


def call(body, name, out_shape, inputs=0, flops=0, moved=1 << 20, **more):
    return pl.pallas_call(
        body,
        name=name,
        in_specs=[VMEM] * inputs,
        out_shape=out_shape,
        compiler_params=pltpu.CompilerParams(vmem_limit_bytes=20 << 20),
        cost_estimate=pl.CostEstimate(flops=flops, bytes_accessed=moved, transcendentals=0),
        **more,
    )


def shaped(shape, dtype):
    return jax.ShapeDtypeStruct(shape, dtype)


def mm(a, b, dims=((1,), (0,))):
    return lax.dot_general(a, b, (dims, ((), ())), preferred_element_type=F32)


def pattern(rows, lanes):
    return (rows == lanes).astype(F32).astype(BF16)


def here():
    row, block = lax.axis_index("row"), lax.axis_index("blk")
    sides = lax.axis_size("blk") // 2
    return block % 2, (row % 2) * sides + block // 2, row // 2, block


def part(ref, core):
    half = ref.shape[1] // 2
    return ref[:, pl.ds(pl.multiple_of(core * half, half), half)]


def inverse(links_ref, width):
    return 1.0 / links_ref[links_ref.shape[0] - 1 :, 0:width].astype(F32)


def linked(column, s_ref):
    lanes = lax.broadcasted_iota(jnp.int32, (column.shape[0], s_ref.shape[0]), 1)
    return mm(pattern(column, lanes), s_ref[...])


def gather_first(links0_ref, links1_ref, s_ref, t_ref, ws_ref, columns_ref, own_ref, h_ref, weight_ref, near_ref):
    core, _, _, block = here()
    rows = t_ref.shape[0]
    weight = part(ws_ref, core)
    weight_ref[...] = weight
    own_ref[...] = mm(t_ref[...], weight)
    for i, links_ref in enumerate((links0_ref, links1_ref)):
        span = pl.ds(i * rows, rows)
        for m in range(near_ref.shape[0]):
            near_ref[m : m + 1, :] = links_ref[pl.ds(block ^ m, 1), :]
        columns = near_ref[...].T
        columns_ref[span, :] = columns
        h_ref[span, :] = linked(columns[:, 0:1], s_ref)


def gather_more(order, columns_ref, h0_ref, t_ref, weight_ref, *refs):
    s_refs, own_ref, h_ref = refs[:-2], refs[-2], refs[-1]
    own_ref[...] = mm(t_ref[...], weight_ref[...])
    rows = t_ref.shape[0]
    for i in range(2):
        span = pl.ds(i * rows, rows)
        total = h0_ref[span, :]
        for m, s_ref in zip(order, s_refs):
            total = total + linked(columns_ref[span, m : m + 1], s_ref)
        h_ref[span, :] = total


def forward(order, links0_ref, links1_ref, columns_ref, h0_ref, own0_ref, own1_ref, wm_ref, t0_ref, t1_ref, c0_ref, c1_ref, *refs):
    s_refs, (h_ref, grad_ref, *updated_refs) = refs[:-4], refs[-4:]
    core = here()[0]
    rows, width = t0_ref.shape
    weight = part(wm_ref, core)
    sides = ((links0_ref, t0_ref, c0_ref, own0_ref), (links1_ref, t1_ref, c1_ref, own1_ref))
    for i, (links_ref, t_ref, c_ref, own_ref) in enumerate(sides):
        span = pl.ds(i * rows, rows)
        total = h0_ref[span, :]
        for m, s_ref in zip(order, s_refs):
            total = total + linked(columns_ref[span, m : m + 1], s_ref)
        gathered = (total * inverse(links_ref, width)).astype(BF16)
        h_ref[span, :] = gathered
        preact = own_ref[...] + mm(gathered, weight)
        sig = jax.nn.sigmoid(preact)
        updated_refs[i][...] = (part(t_ref, core).astype(F32) + preact * sig).astype(BF16)
        upstream = part(c_ref, core).astype(F32)
        grad_ref[span, :] = (upstream * sig * (1.0 + preact * (1.0 - sig))).astype(BF16)


def weight_terms(t0_ref, t1_ref, h_ref, grad_ref, *refs):
    own_ref, sent_refs, total_ref = refs[0], refs[1:-1], refs[-1]
    quad = here()[1]
    rows, width = t0_ref.shape
    piece = own_ref.shape[0]
    total_ref[0:width, :] = mm(t0_ref[...], grad_ref[0:rows, :], ROWS) + mm(t1_ref[...], grad_ref[rows:, :], ROWS)
    total_ref[width:, :] = mm(h_ref[...], grad_ref[...], ROWS)
    for m, ref in enumerate((own_ref, *sent_refs)):
        at = pl.multiple_of((quad ^ m) * piece, piece)
        ref[...] = total_ref[pl.ds(at, piece), :].astype(ref.dtype)


def source_terms(share, sides, orders, links0_ref, links1_ref, grad_ref, other_ref, *refs):
    core, quad, layer, _ = here()
    targets = links0_ref.shape[1]
    half = grad_ref.shape[1]
    rows = 2 * refs[0].shape[0] // len(orders[0])
    position = lax.broadcasted_iota(jnp.int32, (rows, targets), 0)
    inverses = [inverse(ref, half) for ref in (links0_ref, links1_ref)]
    for n, order in enumerate(orders):
        far = position // share + n * (rows // share)
        inside = (layer ^ far) * (2 * share) + position % share
        for j, m in enumerate(order):
            ref = refs[2 * n + j // (len(order) // 2)]
            at = (j % (len(order) // 2)) * rows
            to = quad ^ m
            row_at = inside + (to // sides) * share
            block = (to % sides) * 2 + core
            totals = [None, None]
            for i, links_ref in enumerate((links0_ref, links1_ref)):
                chosen = pattern(links_ref[pl.ds(block, 1), :], row_at)
                for c, g_ref in enumerate((grad_ref, other_ref)):
                    at_target = (i ^ c) * targets
                    added = mm(chosen, g_ref[at_target : at_target + targets, :]) * inverses[i]
                    totals[c] = added if totals[c] is None else totals[c] + added
            first = core == 0
            ref[at : at + rows, 0:half] = jnp.where(first, totals[0], totals[1]).astype(ref.dtype)
            ref[at : at + rows, half:] = jnp.where(first, totals[1], totals[0]).astype(ref.dtype)


def halve(own_ref, received_ref, *refs):
    rows = refs[0].shape[0]
    for n, ref in enumerate(refs):
        span = pl.ds(n * rows, rows)
        ref[...] = (own_ref[span, :] + received_ref[span, :].astype(F32)).astype(ref.dtype)


def add_up(*refs):
    total = refs[0][...].astype(F32)
    for ref in refs[1:-1]:
        total = total + ref[...].astype(F32)
    refs[-1][...] = total.astype(BF16)


def finish_source(wm_ref, own_ref, received_ref, out_ref):
    total = (own_ref[...] + received_ref[...].astype(F32)).astype(BF16)
    out_ref[...] = mm(total, wm_ref[...], LANES).astype(BF16)


def target_side(ws_ref, cot_ref, grad_ref, grad_received_ref, held_ref, held_received_ref, out_ref, updated_ref):
    core = here()[0]
    rows = cot_ref.shape[0]
    out_ref[...] = (
        cot_ref[...].astype(F32)
        + mm(grad_ref[0:rows, :], part(ws_ref, core), LANES)
        + mm(grad_received_ref[rows:, :], part(ws_ref, 1 - core), LANES)
    ).astype(BF16)
    half = held_ref.shape[1]
    updated_ref[:, pl.ds(pl.multiple_of(core * half, half), half)] = held_ref[...]
    updated_ref[:, pl.ds(pl.multiple_of((1 - core) * half, half), half)] = held_received_ref[...]


def finish_weights(quads, scales, *refs):
    refs, outs, buffer, sems = refs[: 2 * quads], refs[-4:-2], refs[-2], refs[-1]
    core, quad, _, _ = here()
    count = quads // 2
    rows, half = refs[0].shape

    def copies(n):
        slot = quad ^ (n % quads)
        column = pl.multiple_of((core if n < quads else 1 - core) * half, half)
        row = pl.multiple_of((slot % count) * rows, rows)
        return slot // count, [
            pltpu.make_async_copy(buffer.at[n], out.at[pl.ds(row, rows), pl.ds(column, half)], sems.at[n]) for out in outs
        ]

    for n, ref in enumerate(refs):
        which, pair = copies(n)
        buffer[n] = ref[...].astype(F32) * jnp.where(which == 0, scales[0], scales[1])
        for k in range(2):
            pl.when(which == k)(pair[k].start)
    for n in range(2 * quads):
        which, pair = copies(n)
        for k in range(2):
            pl.when(which == k)(pair[k].wait)


def local(row_devices, blk_devices, source_table, target_table, message_weight, self_weight, tile_lists, key_offsets, list_lengths, cotangent):
    devices = row_devices * blk_devices
    targets, width = target_table.shape
    block_rows = source_table.shape[0]
    slots = tile_lists.shape[1]
    assert tile_lists.shape[0] == 1 and block_rows == targets and slots == blk_devices
    half = width // 2
    sides = blk_devices // 2
    quads = blk_devices
    layers = row_devices // 2
    share = block_rows // row_devices
    square = 2 * targets * width * width

    direct = list(range(2, blk_devices, 2))
    held = {m: swap(source_table, m, devices) for m in direct}

    blocks = lax.iota(jnp.int32, blk_devices)
    used = (tile_lists[0][None, :] == blocks[:, None]) & (lax.iota(jnp.int32, slots)[None, :] < list_lengths[0])
    links = jnp.max(jnp.where(used[:, :, None], key_offsets.T[None, :, :], -1), axis=1)
    links = jnp.concatenate([links, jnp.broadcast_to(list_lengths[:, None], (8 - slots % 8, targets))], axis=0)
    their_links = swap(links, 1, devices)

    table0, cot0 = target_table, cotangent
    held[1] = swap(source_table, 1, devices)
    table1 = swap(table0, 1, devices)
    cot1 = swap(cot0, 1, devices)

    columns, own0, gathered, weight = call(
        gather_first,
        "gather_first",
        (
            shaped((2 * targets, slots), jnp.int32),
            shaped((targets, half), F32),
            shaped((2 * targets, width), F32),
            shaped((width, half), BF16),
        ),
        inputs=5,
        moved=0,
        scratch_shapes=[pltpu.VMEM((slots, targets), jnp.int32)],
    )(links, their_links, source_table, table0, self_weight)
    ready = lax.optimization_barrier((columns, own0, gathered, weight, *[held[m] for m in direct]))
    columns, own0, gathered, weight = ready[:4]
    for m, value in zip(direct, ready[4:]):
        held[m] = value
        held[m + 1] = swap(value, 1, devices)
    order = [1, *direct]
    own1, gathered = call(
        functools.partial(gather_more, order),
        "gather_more",
        (shaped((targets, half), F32), shaped((2 * targets, width), F32)),
        inputs=4 + len(order),
        flops=2 * square,
    )(columns, gathered, table1, weight, *[held[m] for m in order])
    order = [m + 1 for m in direct]
    gathered, grad, updated, updated_there = call(
        functools.partial(forward, order),
        "forward",
        (shaped((2 * targets, width), BF16), shaped((2 * targets, half), BF16)) + (shaped((targets, half), BF16),) * 2,
        inputs=11 + len(order),
        flops=2 * sides * square,
    )(
        links, their_links, columns, gathered, own0, own1, message_weight, table0, table1, cot0, cot1,
        *[held[m] for m in order],
    )

    piece = 2 * width // quads
    terms = call(
        weight_terms,
        "weight_terms",
        [shaped((piece, half), F32)] + [shaped((piece, half), BF16)] * (quads - 1),
        inputs=4,
        flops=2 * square,
        scratch_shapes=[pltpu.VMEM((2 * width, half), F32)],
    )(table0, table1, gathered, grad)
    received = [swap(terms[m], 2 * m, devices) for m in reversed(range(1, quads))]

    terms, grad_sent, updated_there = lax.optimization_barrier((terms, grad, updated_there))
    grad_received = swap(grad_sent, 1, devices)
    updated_received = swap(updated_there, 1, devices)
    masks = [1 << i for i in range(quads.bit_length() - 1)]
    routes = (masks, masks[::-1])
    orders = [[sum(mask * ((j >> (len(masks) - 1 - i)) & 1) for i, mask in enumerate(route)) for j in range(quads)] for route in routes]
    half_rows = layers * share // 2
    count = quads // 2 * half_rows
    terms, grad_received = lax.optimization_barrier((terms, grad_received))
    sources = call(
        functools.partial(source_terms, share, sides, orders),
        "source_terms",
        [shaped((count, width), F32), shaped((count, width), BF16)] * 2,
        inputs=4,
        flops=4 * square,
    )(links, their_links, grad, grad_received)
    _, received = lax.optimization_barrier((sources, received))

    state = [[sources[0], sources[1]], [sources[2], sources[3]]]

    def source_step(n):
        return [swap(state[k][1], 2 * routes[k][n], devices) for k in range(2)]

    def source_add(n, came):
        for k in range(2):
            if n == len(masks) - 1:
                outs = [shaped((half_rows, width), (F32, BF16)[k])]
            else:
                rows = state[k][0].shape[0] // 2
                outs = [shaped((rows, width), F32), shaped((rows, width), BF16)]
            state[k] = call(halve, "source_sum", outs, inputs=2)(state[k][0], came[k])

    total = call(add_up, "weight_sum", shaped((piece, half), BF16), inputs=quads)(terms[0], *received)
    mask, n = 1, 0
    while mask < layers:
        other = swap(total, 2 * quads * mask, devices)
        came = source_step(n)
        if mask == 1:
            target_gradient, updated = call(
                target_side, "target_side", (shaped((targets, width), BF16),) * 2, inputs=6, flops=square
            )(self_weight, cot0, grad, grad_received, updated, updated_received)
            other, target_gradient, updated = lax.optimization_barrier((other, target_gradient, updated))
        total = call(add_up, "weight_sum", shaped((piece, half), BF16), inputs=2)(total, other)
        source_add(n, came)
        mask, n = 2 * mask, n + 1
    while n < len(masks):
        source_add(n, source_step(n))
        n += 1
    stays, goes = state[0][0], state[1][0]
    pieces = {0: total}
    for m in reversed(range(1, quads)):
        pieces[m] = swap(total, 2 * m, devices)

    mask = layers
    while mask > 1:
        mask //= 2
        came = swap(goes, 2 * quads * mask, devices)
        if mask == 1:
            source_gradient = call(finish_source, "finish_source", shaped((share, width), BF16), inputs=3)(
                message_weight, stays, came
            )
        else:
            rows = stays.shape[0] // 2
            stays, goes = call(halve, "source_sum", [shaped((rows, width), F32), shaped((rows, width), BF16)], inputs=2)(
                stays, came
            )

    their_pieces = {m: swap(value, 1, devices) for m, value in pieces.items()}
    scales = ((targets * devices) ** (-0.5), (block_rows * blk_devices) ** (-0.5))
    self_gradient, message_gradient = call(
        functools.partial(finish_weights, quads, scales),
        "finish_weights",
        (shaped((width, width), F32),) * 2,
        inputs=2 * quads,
        out_specs=(HBM, HBM),
        scratch_shapes=[pltpu.VMEM((2 * quads, piece, half), F32), pltpu.SemaphoreType.DMA((2 * quads,))],
    )(*[values[m] for values in (pieces, their_pieces) for m in range(quads)])
    return (updated, target_gradient, source_gradient, self_gradient, message_gradient)


def solution(mesh):
    split = P(AXES, None)
    return jax.shard_map(
        functools.partial(local, mesh.shape["row"], mesh.shape["blk"]),
        mesh=mesh,
        in_specs=(P("blk", None), split, P(), P(), split, split, P(AXES), split),
        out_specs=(split, split, P(("blk", "row"), None), P(), P()),
        check_vma=False,
    )
```

```python
import functools

import jax
import jax.numpy as jnp
from jax import lax
from jax.experimental import pallas as pl
from jax.experimental.pallas import tpu as pltpu
from jax.sharding import PartitionSpec as P

AXES = ("row", "blk")
BF16 = jnp.bfloat16
F32 = jnp.float32
VMEM = pl.BlockSpec(memory_space=pltpu.VMEM)
HBM = pl.BlockSpec(memory_space=pltpu.HBM)
ROWS = ((0,), (0,))
LANES = ((1,), (1,))


def swap(value, mask, devices):
    return lax.ppermute(value, AXES, [(i, i ^ mask) for i in range(devices)])


def call(body, name, out_shape, inputs=0, flops=0, moved=1 << 20, **more):
    return pl.pallas_call(
        body,
        name=name,
        in_specs=[VMEM] * inputs,
        out_shape=out_shape,
        compiler_params=pltpu.CompilerParams(vmem_limit_bytes=20 << 20),
        cost_estimate=pl.CostEstimate(flops=0, bytes_accessed=0, transcendentals=0),
        **more,
    )


def shaped(shape, dtype):
    return jax.ShapeDtypeStruct(shape, dtype)


def mm(a, b, dims=((1,), (0,))):
    return lax.dot_general(a, b, (dims, ((), ())), preferred_element_type=F32)


def pattern(rows, lanes):
    return (rows == lanes).astype(F32).astype(BF16)


def here():
    row, block = lax.axis_index("row"), lax.axis_index("blk")
    sides = lax.axis_size("blk") // 2
    return block % 2, (row % 2) * sides + block // 2, row // 2, block


def part(ref, core):
    half = ref.shape[1] // 2
    return ref[:, pl.ds(pl.multiple_of(core * half, half), half)]


def inverse(links_ref, width):
    return 1.0 / links_ref[links_ref.shape[0] - 1 :, 0:width].astype(F32)


def linked(column, s_ref):
    lanes = lax.broadcasted_iota(jnp.int32, (column.shape[0], s_ref.shape[0]), 1)
    return mm(pattern(column, lanes), s_ref[...])


def gather_first(links0_ref, links1_ref, s_ref, t_ref, ws_ref, columns_ref, own_ref, h_ref, weight_ref, near_ref):
    core, _, _, block = here()
    rows = t_ref.shape[0]
    weight = part(ws_ref, core)
    weight_ref[...] = weight
    own_ref[...] = mm(t_ref[...], weight)
    for i, links_ref in enumerate((links0_ref, links1_ref)):
        span = pl.ds(i * rows, rows)
        for m in range(near_ref.shape[0]):
            near_ref[m : m + 1, :] = links_ref[pl.ds(block ^ m, 1), :]
        columns = near_ref[...].T
        columns_ref[span, :] = columns
        h_ref[span, :] = linked(columns[:, 0:1], s_ref)


def gather_more(order, columns_ref, h0_ref, t_ref, weight_ref, *refs):
    s_refs, own_ref, h_ref = refs[:-2], refs[-2], refs[-1]
    own_ref[...] = mm(t_ref[...], weight_ref[...])
    rows = t_ref.shape[0]
    for i in range(2):
        span = pl.ds(i * rows, rows)
        total = h0_ref[span, :]
        for m, s_ref in zip(order, s_refs):
            total = total + linked(columns_ref[span, m : m + 1], s_ref)
        h_ref[span, :] = total


def forward(order, links0_ref, links1_ref, columns_ref, h0_ref, own0_ref, own1_ref, wm_ref, t0_ref, t1_ref, c0_ref, c1_ref, *refs):
    s_refs, (h_ref, grad_ref, *updated_refs) = refs[:-4], refs[-4:]
    core = here()[0]
    rows, width = t0_ref.shape
    weight = part(wm_ref, core)
    sides = ((links0_ref, t0_ref, c0_ref, own0_ref), (links1_ref, t1_ref, c1_ref, own1_ref))
    for i, (links_ref, t_ref, c_ref, own_ref) in enumerate(sides):
        span = pl.ds(i * rows, rows)
        total = h0_ref[span, :]
        for m, s_ref in zip(order, s_refs):
            total = total + linked(columns_ref[span, m : m + 1], s_ref)
        gathered = (total * inverse(links_ref, width)).astype(BF16)
        h_ref[span, :] = gathered
        preact = own_ref[...] + mm(gathered, weight)
        sig = jax.nn.sigmoid(preact)
        updated_refs[i][...] = (part(t_ref, core).astype(F32) + preact * sig).astype(BF16)
        upstream = part(c_ref, core).astype(F32)
        grad_ref[span, :] = (upstream * sig * (1.0 + preact * (1.0 - sig))).astype(BF16)


def weight_terms(t0_ref, t1_ref, h_ref, grad_ref, *refs):
    own_ref, sent_refs, total_ref = refs[0], refs[1:-1], refs[-1]
    quad = here()[1]
    rows, width = t0_ref.shape
    piece = own_ref.shape[0]
    total_ref[0:width, :] = mm(t0_ref[...], grad_ref[0:rows, :], ROWS) + mm(t1_ref[...], grad_ref[rows:, :], ROWS)
    total_ref[width:, :] = mm(h_ref[...], grad_ref[...], ROWS)
    for m, ref in enumerate((own_ref, *sent_refs)):
        at = pl.multiple_of((quad ^ m) * piece, piece)
        ref[...] = total_ref[pl.ds(at, piece), :].astype(ref.dtype)


def source_terms(share, sides, orders, links0_ref, links1_ref, grad_ref, other_ref, *refs):
    core, quad, layer, _ = here()
    targets = links0_ref.shape[1]
    half = grad_ref.shape[1]
    rows = 2 * refs[0].shape[0] // len(orders[0])
    position = lax.broadcasted_iota(jnp.int32, (rows, targets), 0)
    inverses = [inverse(ref, half) for ref in (links0_ref, links1_ref)]
    for n, order in enumerate(orders):
        far = reverse_bits(position // share + n * (rows // share), 2 * rows // share)
        inside = (layer ^ far) * (2 * share) + position % share
        for j, m in enumerate(order):
            ref = refs[2 * n + j // (len(order) // 2)]
            at = (j % (len(order) // 2)) * rows
            to = quad ^ m
            row_at = inside + (to // sides) * share
            block = (to % sides) * 2 + 1 - core
            totals = [None, None]
            for i, links_ref in enumerate((links0_ref, links1_ref)):
                chosen = pattern(links_ref[pl.ds(block, 1), :], row_at)
                for c, g_ref in enumerate((grad_ref, other_ref)):
                    at_target = (i ^ c) * targets
                    added = mm(chosen, g_ref[at_target : at_target + targets, :]) * inverses[i]
                    totals[c] = added if totals[c] is None else totals[c] + added
            first = core == 0
            ref[at : at + rows, 0:half] = jnp.where(first, totals[0], totals[1]).astype(ref.dtype)
            ref[at : at + rows, half:] = jnp.where(first, totals[1], totals[0]).astype(ref.dtype)


def reverse_bits(value, size):
    result, low, high = value * 0, 1, size // 2
    while high:
        result = result + ((value // low) % 2) * high
        low, high = low * 2, high // 2
    return result


def halve(own_ref, received_ref, *refs):
    rows = refs[0].shape[0]
    for n, ref in enumerate(refs):
        span = pl.ds(n * rows, rows)
        ref[...] = (own_ref[span, :] + received_ref[span, :].astype(F32)).astype(ref.dtype)


def add_up(*refs):
    total = refs[0][...].astype(F32)
    for ref in refs[1:-1]:
        total = total + ref[...].astype(F32)
    refs[-1][...] = total.astype(BF16)


def target_side(ws_ref, cot_ref, grad_ref, grad_received_ref, held_ref, held_received_ref, out_ref, updated_ref):
    core = here()[0]
    rows = cot_ref.shape[0]
    out_ref[...] = (
        cot_ref[...].astype(F32)
        + mm(grad_ref[0:rows, :], part(ws_ref, core), LANES)
        + mm(grad_received_ref[rows:, :], part(ws_ref, 1 - core), LANES)
    ).astype(BF16)
    half = held_ref.shape[1]
    updated_ref[:, pl.ds(pl.multiple_of(core * half, half), half)] = held_ref[...]
    updated_ref[:, pl.ds(pl.multiple_of((1 - core) * half, half), half)] = held_received_ref[...]


def project_back(total_ref, wm_ref, out_ref):
    out_ref[...] = mm(total_ref[...], wm_ref[...], LANES).astype(BF16)


def finish(quads, scales, rows_ref, *refs):
    refs, outs, (buffer, sems) = refs[: 2 * quads], refs[2 * quads : 2 * quads + 3], refs[2 * quads + 3 :]
    core, quad, _, _ = here()
    count = quads // 2
    rows, half = refs[0].shape

    def copies(n):
        slot = quad ^ (n % quads)
        column = pl.multiple_of((core if n < quads else 1 - core) * half, half)
        row = pl.multiple_of((slot % count) * rows, rows)
        return slot // count, [
            pltpu.make_async_copy(buffer.at[n], out.at[pl.ds(row, rows), pl.ds(column, half)], sems.at[n])
            for out in outs[:2]
        ]

    last = pltpu.make_async_copy(rows_ref, outs[2], sems.at[2 * quads])
    last.start()
    for n, ref in enumerate(refs):
        which, pair = copies(n)
        buffer[n] = ref[...].astype(F32) * jnp.where(which == 0, scales[0], scales[1])
        for k in range(2):
            pl.when(which == k)(pair[k].start)
    for n in range(2 * quads):
        which, pair = copies(n)
        for k in range(2):
            pl.when(which == k)(pair[k].wait)
    last.wait()


def local(row_devices, blk_devices, source_table, target_table, message_weight, self_weight, tile_lists, key_offsets, list_lengths, cotangent):
    devices = row_devices * blk_devices
    targets, width = target_table.shape
    block_rows = source_table.shape[0]
    slots = tile_lists.shape[1]
    assert tile_lists.shape[0] == 1 and block_rows == targets and slots == blk_devices
    half = width // 2
    sides = blk_devices // 2
    quads = blk_devices
    layers = row_devices // 2
    share = block_rows // row_devices
    square = 2 * targets * width * width

    direct = list(range(2, blk_devices, 2))
    held = {m: swap(source_table, m, devices) for m in direct}

    blocks = lax.iota(jnp.int32, blk_devices)
    used = (tile_lists[0][None, :] == blocks[:, None]) & (lax.iota(jnp.int32, slots)[None, :] < list_lengths[0])
    links = jnp.max(jnp.where(used[:, :, None], key_offsets.T[None, :, :], -1), axis=1)
    links = jnp.concatenate([links, jnp.broadcast_to(list_lengths[:, None], (8 - slots % 8, targets))], axis=0)
    their_links = swap(links, 1, devices)

    table0, cot0 = target_table, cotangent
    held[1] = swap(source_table, 1, devices)
    table1 = swap(table0, 1, devices)
    cot1 = swap(cot0, 1, devices)

    columns, own0, gathered, weight = call(
        gather_first,
        "gather_first",
        (
            shaped((2 * targets, slots), jnp.int32),
            shaped((targets, half), F32),
            shaped((2 * targets, width), F32),
            shaped((width, half), BF16),
        ),
        inputs=5,
        moved=0,
        scratch_shapes=[pltpu.VMEM((slots, targets), jnp.int32)],
    )(links, their_links, source_table, table0, self_weight)
    ready = lax.optimization_barrier((columns, own0, gathered, weight, *[held[m] for m in direct]))
    columns, own0, gathered, weight = ready[:4]
    for m, value in zip(direct, ready[4:]):
        held[m] = value
        held[m + 1] = swap(value, 1, devices)
    order = [1, *direct]
    own1, gathered = call(
        functools.partial(gather_more, order),
        "gather_more",
        (shaped((targets, half), F32), shaped((2 * targets, width), F32)),
        inputs=4 + len(order),
        flops=2 * square,
    )(columns, gathered, table1, weight, *[held[m] for m in order])
    order = [m + 1 for m in direct]
    gathered, grad, updated, updated_there = call(
        functools.partial(forward, order),
        "forward",
        (shaped((2 * targets, width), BF16), shaped((2 * targets, half), BF16)) + (shaped((targets, half), BF16),) * 2,
        inputs=11 + len(order),
        flops=2 * sides * square,
    )(
        links, their_links, columns, gathered, own0, own1, message_weight, table0, table1, cot0, cot1,
        *[held[m] for m in order],
    )

    piece = 2 * width // quads
    terms = call(
        weight_terms,
        "weight_terms",
        [shaped((piece, half), F32)] + [shaped((piece, half), BF16)] * (quads - 1),
        inputs=4,
        flops=2 * square,
        scratch_shapes=[pltpu.VMEM((2 * width, half), F32)],
    )(table0, table1, gathered, grad)
    received = [swap(terms[m], 2 * m, devices) for m in reversed(range(1, quads))]

    terms, grad_sent, updated_there = lax.optimization_barrier((terms, grad, updated_there))
    grad_received = swap(grad_sent, 1, devices)
    updated_received = swap(updated_there, 1, devices)
    masks = [1 << i for i in range(quads.bit_length() - 1)]
    routes = (masks, masks[::-1])
    orders = [[sum(mask * ((j >> (len(masks) - 1 - i)) & 1) for i, mask in enumerate(route)) for j in range(quads)] for route in routes]
    half_rows = layers * share // 2
    count = quads // 2 * half_rows
    terms, grad_received = lax.optimization_barrier((terms, grad_received))
    sources = call(
        functools.partial(source_terms, share, sides, orders),
        "source_terms",
        [shaped((count, width), F32), shaped((count, width), BF16)] * 2,
        inputs=4,
        flops=4 * square,
    )(links, their_links, grad, grad_received)
    target_gradient, updated = call(
        target_side, "target_side", (shaped((targets, width), BF16),) * 2, inputs=6
    )(self_weight, cot0, grad, grad_received, updated, updated_received)
    _, received, target_gradient, updated = lax.optimization_barrier((sources, received, target_gradient, updated))

    state = [[sources[0], sources[1]], [sources[2], sources[3]]]

    def source_step(n):
        return [swap(state[k][1], 2 * routes[k][n], devices) for k in range(2)]

    def source_add(n, came):
        for k in range(2):
            if n == len(masks) - 1:
                outs = [shaped((half_rows, width), (F32, BF16)[k])]
            else:
                rows = state[k][0].shape[0] // 2
                outs = [shaped((rows, width), F32), shaped((rows, width), BF16)]
            state[k] = call(halve, "source_sum", outs, inputs=2)(state[k][0], came[k])

    total = call(add_up, "weight_sum", shaped((piece, half), BF16), inputs=quads)(terms[0], *received)
    mask, n = 1, 0
    while mask < layers:
        other = swap(total, 2 * quads * mask, devices)
        came = source_step(n)
        total = call(add_up, "weight_sum", shaped((piece, half), BF16), inputs=2)(total, other)
        source_add(n, came)
        mask, n = 2 * mask, n + 1
    while n < len(masks):
        source_add(n, source_step(n))
        n += 1
    stays, goes = state[0][0], state[1][0]
    total = lax.optimization_barrier((total, goes))[0]
    pieces = {0: total}
    for m in reversed(range(1, quads)):
        pieces[m] = swap(total, 2 * m, devices)

    mask = 1
    while mask < layers:
        came = swap(goes, 2 * quads * mask, devices)
        mask *= 2
        if mask == layers:
            rounded = call(halve, "source_sum", [shaped((share, width), BF16)], inputs=2)(stays, came)[0]
            source_rows = call(project_back, "project_back", pltpu.VMEM((share, width), BF16), inputs=2)(
                swap(rounded, 1, devices), message_weight
            )
        else:
            rows = stays.shape[0] // 2
            stays, goes = call(halve, "source_sum", [shaped((rows, width), F32), shaped((rows, width), BF16)], inputs=2)(
                stays, came
            )

    their_pieces = {m: swap(value, 1, devices) for m, value in pieces.items()}
    scales = ((targets * devices) ** (-0.5), (block_rows * blk_devices) ** (-0.5))
    self_gradient, message_gradient, source_gradient = call(
        functools.partial(finish, quads, scales),
        "finish",
        (shaped((width, width), F32),) * 2 + (shaped((share, width), BF16),),
        inputs=1 + 2 * quads,
        out_specs=(HBM, HBM, HBM),
        scratch_shapes=[
            pltpu.VMEM((2 * quads, piece, half), F32),
            pltpu.SemaphoreType.DMA((2 * quads + 1,)),
        ],
    )(source_rows, *[values[m] for values in (pieces, their_pieces) for m in range(quads)])
    return (updated, target_gradient, source_gradient, self_gradient, message_gradient)


def solution(mesh):
    split = P(AXES, None)
    return jax.shard_map(
        functools.partial(local, mesh.shape["row"], mesh.shape["blk"]),
        mesh=mesh,
        in_specs=(P("blk", None), split, P(), P(), split, split, P(AXES), split),
        out_specs=(split, split, P(("blk", "row"), None), P(), P()),
        check_vma=False,
    )
```

```python
import functools

import jax
import jax.numpy as jnp
from jax import lax
from jax.experimental import pallas as pl
from jax.experimental.pallas import tpu as pltpu
from jax.sharding import PartitionSpec as P

AXES = ("row", "blk")
BF16 = jnp.bfloat16
F32 = jnp.float32
VMEM = pl.BlockSpec(memory_space=pltpu.VMEM)
HBM = pl.BlockSpec(memory_space=pltpu.HBM)
ROWS = ((0,), (0,))
LANES = ((1,), (1,))


def swap(value, mask, devices):
    return lax.ppermute(value, AXES, [(i, i ^ mask) for i in range(devices)])


def call(body, name, out_shape, inputs=0, flops=0, moved=1 << 20, **more):
    return pl.pallas_call(
        body,
        name=name,
        in_specs=[VMEM] * inputs,
        out_shape=out_shape,
        compiler_params=pltpu.CompilerParams(vmem_limit_bytes=20 << 20),
        cost_estimate=pl.CostEstimate(flops=0, bytes_accessed=0, transcendentals=0),
        **more,
    )


def shaped(shape, dtype):
    return jax.ShapeDtypeStruct(shape, dtype)


def mm(a, b, dims=((1,), (0,))):
    return lax.dot_general(a, b, (dims, ((), ())), preferred_element_type=F32)


def pattern(rows, lanes):
    return (rows == lanes).astype(F32).astype(BF16)


def here():
    row, block = lax.axis_index("row"), lax.axis_index("blk")
    sides = lax.axis_size("blk") // 2
    return block % 2, (row % 2) * sides + block // 2, row // 2, block


def part(ref, core):
    half = ref.shape[1] // 2
    return ref[:, pl.ds(pl.multiple_of(core * half, half), half)]


def inverse(links_ref, width):
    return 1.0 / links_ref[links_ref.shape[0] - 1 :, 0:width].astype(F32)


def linked(column, s_ref):
    lanes = lax.broadcasted_iota(jnp.int32, (column.shape[0], s_ref.shape[0]), 1)
    return mm(pattern(column, lanes), s_ref[...])


def gather_first(links0_ref, links1_ref, s_ref, t_ref, ws_ref, columns_ref, own_ref, h_ref, weight_ref, near_ref):
    core, _, _, block = here()
    rows = t_ref.shape[0]
    weight = part(ws_ref, core)
    weight_ref[...] = weight
    own_ref[...] = mm(t_ref[...], weight)
    for i, links_ref in enumerate((links0_ref, links1_ref)):
        span = pl.ds(i * rows, rows)
        for m in range(near_ref.shape[0]):
            near_ref[m : m + 1, :] = links_ref[pl.ds(block ^ m, 1), :]
        columns = near_ref[...].T
        columns_ref[span, :] = columns
        h_ref[span, :] = linked(columns[:, 0:1], s_ref)


def gather_more(order, columns_ref, h0_ref, t_ref, weight_ref, *refs):
    s_refs, own_ref, h_ref = refs[:-2], refs[-2], refs[-1]
    own_ref[...] = mm(t_ref[...], weight_ref[...])
    rows = t_ref.shape[0]
    for i in range(2):
        span = pl.ds(i * rows, rows)
        total = h0_ref[span, :]
        for m, s_ref in zip(order, s_refs):
            total = total + linked(columns_ref[span, m : m + 1], s_ref)
        h_ref[span, :] = total


def forward(order, links0_ref, links1_ref, columns_ref, h0_ref, own0_ref, own1_ref, wm_ref, t0_ref, t1_ref, c0_ref, c1_ref, *refs):
    s_refs, (h_ref, grad_ref, updated_ref) = refs[:-3], refs[-3:]
    core = here()[0]
    rows, width = t0_ref.shape
    weight = part(wm_ref, core)
    sides = ((links0_ref, t0_ref, c0_ref, own0_ref), (links1_ref, t1_ref, c1_ref, own1_ref))
    for i, (links_ref, t_ref, c_ref, own_ref) in enumerate(sides):
        span = pl.ds(i * rows, rows)
        total = h0_ref[span, :]
        for m, s_ref in zip(order, s_refs):
            total = total + linked(columns_ref[span, m : m + 1], s_ref)
        gathered = (total * inverse(links_ref, width)).astype(BF16)
        h_ref[span, :] = gathered
        preact = own_ref[...] + mm(gathered, weight)
        sig = jax.nn.sigmoid(preact)
        updated = (part(t_ref, core).astype(F32) + preact * sig).astype(BF16)
        if i == 0:
            updated_ref[...] = updated
        else:
            grad_ref[2 * rows :, :] = updated
        upstream = part(c_ref, core).astype(F32)
        grad_ref[span, :] = (upstream * sig * (1.0 + preact * (1.0 - sig))).astype(BF16)


def weight_terms(t0_ref, t1_ref, h_ref, grad_ref, *refs):
    own_ref, sent_refs, total_ref = refs[0], refs[1:-1], refs[-1]
    quad = here()[1]
    rows, width = t0_ref.shape
    piece = own_ref.shape[0]
    total_ref[0:width, :] = mm(t0_ref[...], grad_ref[0:rows, :], ROWS) + mm(t1_ref[...], grad_ref[rows : 2 * rows, :], ROWS)
    total_ref[width:, :] = mm(h_ref[...], grad_ref[0 : 2 * rows, :], ROWS)
    for m, ref in enumerate((own_ref, *sent_refs)):
        at = pl.multiple_of((quad ^ m) * piece, piece)
        ref[...] = total_ref[pl.ds(at, piece), :].astype(ref.dtype)


def source_terms(share, sides, orders, links0_ref, links1_ref, grad_ref, other_ref, *refs):
    core, quad, layer, _ = here()
    targets = links0_ref.shape[1]
    half = grad_ref.shape[1]
    rows = 2 * refs[0].shape[0] // len(orders[0])
    position = lax.broadcasted_iota(jnp.int32, (rows, targets), 0)
    inverses = [inverse(ref, half) for ref in (links0_ref, links1_ref)]
    for n, order in enumerate(orders):
        far = reverse_bits(position // share + n * (rows // share), 2 * rows // share)
        inside = (layer ^ far) * (2 * share) + position % share
        for j, m in enumerate(order):
            ref = refs[2 * n + j // (len(order) // 2)]
            at = (j % (len(order) // 2)) * rows
            to = quad ^ m
            row_at = inside + (to // sides) * share
            block = (to % sides) * 2 + 1 - core
            totals = [None, None]
            for i, links_ref in enumerate((links0_ref, links1_ref)):
                chosen = pattern(links_ref[pl.ds(block, 1), :], row_at)
                for c, g_ref in enumerate((grad_ref, other_ref)):
                    at_target = (i ^ c) * targets
                    added = mm(chosen, g_ref[at_target : at_target + targets, :]) * inverses[i]
                    totals[c] = added if totals[c] is None else totals[c] + added
            first = core == 0
            ref[at : at + rows, 0:half] = jnp.where(first, totals[0], totals[1]).astype(ref.dtype)
            ref[at : at + rows, half:] = jnp.where(first, totals[1], totals[0]).astype(ref.dtype)


def reverse_bits(value, size):
    result, low, high = value * 0, 1, size // 2
    while high:
        result = result + ((value // low) % 2) * high
        low, high = low * 2, high // 2
    return result


def halve(own_ref, received_ref, *refs):
    rows = refs[0].shape[0]
    for n, ref in enumerate(refs):
        span = pl.ds(n * rows, rows)
        ref[...] = (own_ref[span, :] + received_ref[span, :].astype(F32)).astype(ref.dtype)


def add_up(*refs):
    total = refs[0][...].astype(F32)
    for ref in refs[1:-1]:
        total = total + ref[...].astype(F32)
    refs[-1][...] = total.astype(BF16)


def target_side(ws_ref, cot_ref, grad_ref, grad_received_ref, held_ref, out_ref, updated_ref):
    core = here()[0]
    rows = cot_ref.shape[0]
    out_ref[...] = (
        cot_ref[...].astype(F32)
        + mm(grad_ref[0:rows, :], part(ws_ref, core), LANES)
        + mm(grad_received_ref[rows : 2 * rows, :], part(ws_ref, 1 - core), LANES)
    ).astype(BF16)
    half = held_ref.shape[1]
    updated_ref[:, pl.ds(pl.multiple_of(core * half, half), half)] = held_ref[...]
    updated_ref[:, pl.ds(pl.multiple_of((1 - core) * half, half), half)] = grad_received_ref[2 * rows :, :]


def project_back(total_ref, wm_ref, out_ref):
    out_ref[...] = mm(total_ref[...], wm_ref[...], LANES).astype(BF16)


def finish(quads, scales, rows_ref, *refs):
    refs, outs, (buffer, sems) = refs[: 2 * quads], refs[2 * quads : 2 * quads + 3], refs[2 * quads + 3 :]
    core, quad, _, _ = here()
    count = quads // 2
    rows, half = refs[0].shape

    def copies(n):
        slot = quad ^ (n % quads)
        column = pl.multiple_of((core if n < quads else 1 - core) * half, half)
        row = pl.multiple_of((slot % count) * rows, rows)
        return slot // count, [
            pltpu.make_async_copy(buffer.at[n], out.at[pl.ds(row, rows), pl.ds(column, half)], sems.at[n])
            for out in outs[:2]
        ]

    last = pltpu.make_async_copy(rows_ref, outs[2], sems.at[2 * quads])
    last.start()
    for n, ref in enumerate(refs):
        which, pair = copies(n)
        buffer[n] = ref[...].astype(F32) * jnp.where(which == 0, scales[0], scales[1])
        for k in range(2):
            pl.when(which == k)(pair[k].start)
    for n in range(2 * quads):
        which, pair = copies(n)
        for k in range(2):
            pl.when(which == k)(pair[k].wait)
    last.wait()


def local(row_devices, blk_devices, source_table, target_table, message_weight, self_weight, tile_lists, key_offsets, list_lengths, cotangent):
    devices = row_devices * blk_devices
    targets, width = target_table.shape
    block_rows = source_table.shape[0]
    slots = tile_lists.shape[1]
    assert tile_lists.shape[0] == 1 and block_rows == targets and slots == blk_devices
    half = width // 2
    sides = blk_devices // 2
    quads = blk_devices
    layers = row_devices // 2
    share = block_rows // row_devices
    square = 2 * targets * width * width

    direct = list(range(2, blk_devices, 2))
    held = {m: swap(source_table, m, devices) for m in direct}

    blocks = lax.iota(jnp.int32, blk_devices)
    used = (tile_lists[0][None, :] == blocks[:, None]) & (lax.iota(jnp.int32, slots)[None, :] < list_lengths[0])
    links = jnp.max(jnp.where(used[:, :, None], key_offsets.T[None, :, :], -1), axis=1)
    links = jnp.concatenate([links, jnp.broadcast_to(list_lengths[:, None], (8 - slots % 8, targets))], axis=0)
    their_links = swap(links, 1, devices)

    table0, cot0 = target_table, cotangent
    held[1] = swap(source_table, 1, devices)
    table1 = swap(table0, 1, devices)
    cot1 = swap(cot0, 1, devices)

    columns, own0, gathered, weight = call(
        gather_first,
        "gather_first",
        (
            shaped((2 * targets, slots), jnp.int32),
            shaped((targets, half), F32),
            shaped((2 * targets, width), F32),
            shaped((width, half), BF16),
        ),
        inputs=5,
        moved=0,
        scratch_shapes=[pltpu.VMEM((slots, targets), jnp.int32)],
    )(links, their_links, source_table, table0, self_weight)
    ready = lax.optimization_barrier((columns, own0, gathered, weight, *[held[m] for m in direct]))
    columns, own0, gathered, weight = ready[:4]
    for m, value in zip(direct, ready[4:]):
        held[m] = value
        held[m + 1] = swap(value, 1, devices)
    order = [1, *direct]
    own1, gathered = call(
        functools.partial(gather_more, order),
        "gather_more",
        (shaped((targets, half), F32), shaped((2 * targets, width), F32)),
        inputs=4 + len(order),
        flops=2 * square,
    )(columns, gathered, table1, weight, *[held[m] for m in order])
    order = [m + 1 for m in direct]
    gathered, grad, updated = call(
        functools.partial(forward, order),
        "forward",
        (shaped((2 * targets, width), BF16), shaped((3 * targets, half), BF16), shaped((targets, half), BF16)),
        inputs=11 + len(order),
        flops=2 * sides * square,
    )(
        links, their_links, columns, gathered, own0, own1, message_weight, table0, table1, cot0, cot1,
        *[held[m] for m in order],
    )

    piece = 2 * width // quads
    terms = call(
        weight_terms,
        "weight_terms",
        [shaped((piece, half), F32)] + [shaped((piece, half), BF16)] * (quads - 1),
        inputs=4,
        flops=2 * square,
        scratch_shapes=[pltpu.VMEM((2 * width, half), F32)],
    )(table0, table1, gathered, grad)
    received = [swap(terms[m], 2 * m, devices) for m in reversed(range(1, quads))]

    terms, grad_sent = lax.optimization_barrier((terms, grad))
    grad_received = swap(grad_sent, 1, devices)
    masks = [1 << i for i in range(quads.bit_length() - 1)]
    routes = (masks, masks[::-1])
    orders = [[sum(mask * ((j >> (len(masks) - 1 - i)) & 1) for i, mask in enumerate(route)) for j in range(quads)] for route in routes]
    half_rows = layers * share // 2
    count = quads // 2 * half_rows
    terms, grad_received = lax.optimization_barrier((terms, grad_received))
    sources = call(
        functools.partial(source_terms, share, sides, orders),
        "source_terms",
        [shaped((count, width), F32), shaped((count, width), BF16)] * 2,
        inputs=4,
        flops=4 * square,
    )(links, their_links, grad, grad_received)
    target_gradient, updated = call(
        target_side, "target_side", (shaped((targets, width), BF16),) * 2, inputs=5
    )(self_weight, cot0, grad, grad_received, updated)
    _, received, target_gradient, updated = lax.optimization_barrier((sources, received, target_gradient, updated))

    state = [[sources[0], sources[1]], [sources[2], sources[3]]]

    def source_step(n):
        return [swap(state[k][1], 2 * routes[k][n], devices) for k in range(2)]

    def source_add(n, came):
        for k in range(2):
            if n == len(masks) - 1:
                outs = [shaped((half_rows, width), (F32, BF16)[k])]
            else:
                rows = state[k][0].shape[0] // 2
                outs = [shaped((rows, width), F32), shaped((rows, width), BF16)]
            state[k] = call(halve, "source_sum", outs, inputs=2)(state[k][0], came[k])

    total = call(add_up, "weight_sum", shaped((piece, half), BF16), inputs=quads)(terms[0], *received)
    mask, n = 1, 0
    while mask < layers:
        other = swap(total, 2 * quads * mask, devices)
        came = source_step(n)
        total = call(add_up, "weight_sum", shaped((piece, half), BF16), inputs=2)(total, other)
        source_add(n, came)
        mask, n = 2 * mask, n + 1
    while n < len(masks):
        source_add(n, source_step(n))
        n += 1
    stays, goes = state[0][0], state[1][0]
    total = lax.optimization_barrier((total, goes))[0]
    pieces = {0: total}
    for m in reversed(range(1, quads)):
        pieces[m] = swap(total, 2 * m, devices)

    mask = 1
    while mask < layers:
        came = swap(goes, 2 * quads * mask, devices)
        mask *= 2
        if mask == layers:
            rounded = call(halve, "source_sum", [shaped((share, width), BF16)], inputs=2)(stays, came)[0]
            source_rows = call(project_back, "project_back", pltpu.VMEM((share, width), BF16), inputs=2)(
                swap(rounded, 1, devices), message_weight
            )
        else:
            rows = stays.shape[0] // 2
            stays, goes = call(halve, "source_sum", [shaped((rows, width), F32), shaped((rows, width), BF16)], inputs=2)(
                stays, came
            )

    their_pieces = {m: swap(value, 1, devices) for m, value in pieces.items()}
    scales = ((targets * devices) ** (-0.5), (block_rows * blk_devices) ** (-0.5))
    self_gradient, message_gradient, source_gradient = call(
        functools.partial(finish, quads, scales),
        "finish",
        (shaped((width, width), F32),) * 2 + (shaped((share, width), BF16),),
        inputs=1 + 2 * quads,
        out_specs=(HBM, HBM, HBM),
        scratch_shapes=[
            pltpu.VMEM((2 * quads, piece, half), F32),
            pltpu.SemaphoreType.DMA((2 * quads + 1,)),
        ],
    )(source_rows, *[values[m] for values in (pieces, their_pieces) for m in range(quads)])
    return (updated, target_gradient, source_gradient, self_gradient, message_gradient)


def solution(mesh):
    split = P(AXES, None)
    return jax.shard_map(
        functools.partial(local, mesh.shape["row"], mesh.shape["blk"]),
        mesh=mesh,
        in_specs=(P("blk", None), split, P(), P(), split, split, P(AXES), split),
        out_specs=(split, split, P(("blk", "row"), None), P(), P()),
        check_vma=False,
    )
```

```python
import functools

import jax
import jax.numpy as jnp
from jax import lax
from jax.experimental import pallas as pl
from jax.experimental.pallas import tpu as pltpu
from jax.sharding import PartitionSpec as P

AXES = ("row", "blk")
BF16 = jnp.bfloat16
F32 = jnp.float32
VMEM = pl.BlockSpec(memory_space=pltpu.VMEM)
HBM = pl.BlockSpec(memory_space=pltpu.HBM)
ROWS = ((0,), (0,))
LANES = ((1,), (1,))


def swap(value, mask, devices):
    return lax.ppermute(value, AXES, [(i, i ^ mask) for i in range(devices)])


def call(body, name, out_shape, inputs=0, flops=0, moved=1 << 20, **more):
    return pl.pallas_call(
        body,
        name=name,
        in_specs=more.pop("in_specs", [VMEM] * inputs),
        out_shape=out_shape,
        compiler_params=pltpu.CompilerParams(vmem_limit_bytes=20 << 20),
        cost_estimate=pl.CostEstimate(flops=0, bytes_accessed=0, transcendentals=0),
        **more,
    )


def shaped(shape, dtype):
    return jax.ShapeDtypeStruct(shape, dtype)


def mm(a, b, dims=((1,), (0,))):
    return lax.dot_general(a, b, (dims, ((), ())), preferred_element_type=F32)


def pattern(rows, lanes):
    return (rows == lanes).astype(F32).astype(BF16)


def here():
    row, block = lax.axis_index("row"), lax.axis_index("blk")
    sides = lax.axis_size("blk") // 2
    return block % 2, (row % 2) * sides + block // 2, row // 2, block


def part(ref, core):
    half = ref.shape[1] // 2
    return ref[:, pl.ds(pl.multiple_of(core * half, half), half)]


def inverse(links_ref, width):
    return 1.0 / links_ref[links_ref.shape[0] - 1 :, 0:width].astype(F32)


def linked(column, s_ref):
    lanes = lax.broadcasted_iota(jnp.int32, (column.shape[0], s_ref.shape[0]), 1)
    return mm(pattern(column, lanes), s_ref[...])


def gather_first(links0_ref, links1_ref, s_ref, t_ref, ws_ref, columns_ref, own_ref, h_ref, weight_ref, near_ref):
    core, _, _, block = here()
    rows = t_ref.shape[0]
    weight = part(ws_ref, core)
    weight_ref[...] = weight
    own_ref[...] = mm(t_ref[...], weight)
    for i, links_ref in enumerate((links0_ref, links1_ref)):
        span = pl.ds(i * rows, rows)
        for m in range(near_ref.shape[0]):
            near_ref[m : m + 1, :] = links_ref[pl.ds(block ^ m, 1), :]
        columns = near_ref[...].T
        columns_ref[span, :] = columns
        h_ref[span, :] = linked(columns[:, 0:1], s_ref)


def gather_more(order, columns_ref, h0_ref, t_ref, weight_ref, *refs):
    s_refs, own_ref, h_ref = refs[:-2], refs[-2], refs[-1]
    own_ref[...] = mm(t_ref[...], weight_ref[...])
    rows = t_ref.shape[0]
    for i in range(2):
        span = pl.ds(i * rows, rows)
        total = h0_ref[span, :]
        for m, s_ref in zip(order, s_refs):
            total = total + linked(columns_ref[span, m : m + 1], s_ref)
        h_ref[span, :] = total


def forward(order, links0_ref, links1_ref, columns_ref, h0_ref, own0_ref, own1_ref, wm_ref, t0_ref, t1_ref, c0_ref, c1_ref, *refs):
    s_refs, (h_ref, grad_ref, *updated_refs) = refs[:-4], refs[-4:]
    core = here()[0]
    rows, width = t0_ref.shape
    weight = part(wm_ref, core)
    sides = ((links0_ref, t0_ref, c0_ref, own0_ref), (links1_ref, t1_ref, c1_ref, own1_ref))
    for i, (links_ref, t_ref, c_ref, own_ref) in enumerate(sides):
        span = pl.ds(i * rows, rows)
        total = h0_ref[span, :]
        for m, s_ref in zip(order, s_refs):
            total = total + linked(columns_ref[span, m : m + 1], s_ref)
        gathered = (total * inverse(links_ref, width)).astype(BF16)
        h_ref[span, :] = gathered
        preact = own_ref[...] + mm(gathered, weight)
        sig = jax.nn.sigmoid(preact)
        updated_refs[i][...] = (part(t_ref, core).astype(F32) + preact * sig).astype(BF16)
        upstream = part(c_ref, core).astype(F32)
        grad_ref[span, :] = (upstream * sig * (1.0 + preact * (1.0 - sig))).astype(BF16)


def weight_terms(t0_ref, t1_ref, h_ref, grad_ref, *refs):
    own_ref, sent_refs, total_ref = refs[0], refs[1:-1], refs[-1]
    quad = here()[1]
    rows, width = t0_ref.shape
    piece = own_ref.shape[0]
    total_ref[0:width, :] = mm(t0_ref[...], grad_ref[0:rows, :], ROWS) + mm(t1_ref[...], grad_ref[rows:, :], ROWS)
    total_ref[width:, :] = mm(h_ref[...], grad_ref[...], ROWS)
    for m, ref in enumerate((own_ref, *sent_refs)):
        at = pl.multiple_of((quad ^ m) * piece, piece)
        ref[...] = total_ref[pl.ds(at, piece), :].astype(ref.dtype)


def source_terms(share, sides, orders, links0_ref, links1_ref, grad_ref, other_ref, *refs):
    core, quad, layer, _ = here()
    targets = links0_ref.shape[1]
    half = grad_ref.shape[1]
    rows = 2 * refs[0].shape[0] // len(orders[0])
    position = lax.broadcasted_iota(jnp.int32, (rows, targets), 0)
    inverses = [inverse(ref, half) for ref in (links0_ref, links1_ref)]
    for n, order in enumerate(orders):
        far = reverse_bits(position // share + n * (rows // share), 2 * rows // share)
        inside = (layer ^ far) * (2 * share) + position % share
        for j, m in enumerate(order):
            ref = refs[2 * n + j // (len(order) // 2)]
            at = (j % (len(order) // 2)) * rows
            to = quad ^ m
            row_at = inside + (to // sides) * share
            block = (to % sides) * 2 + 1 - core
            totals = [None, None]
            for i, links_ref in enumerate((links0_ref, links1_ref)):
                chosen = pattern(links_ref[pl.ds(block, 1), :], row_at)
                for c, g_ref in enumerate((grad_ref, other_ref)):
                    at_target = (i ^ c) * targets
                    added = mm(chosen, g_ref[at_target : at_target + targets, :]) * inverses[i]
                    totals[c] = added if totals[c] is None else totals[c] + added
            first = core == 0
            ref[at : at + rows, 0:half] = jnp.where(first, totals[0], totals[1]).astype(ref.dtype)
            ref[at : at + rows, half:] = jnp.where(first, totals[1], totals[0]).astype(ref.dtype)


def reverse_bits(value, size):
    result, low, high = value * 0, 1, size // 2
    while high:
        result = result + ((value // low) % 2) * high
        low, high = low * 2, high // 2
    return result


def halve(own_ref, received_ref, *refs):
    rows = refs[0].shape[0]
    for n, ref in enumerate(refs):
        span = pl.ds(n * rows, rows)
        ref[...] = (own_ref[span, :] + received_ref[span, :].astype(F32)).astype(ref.dtype)


def add_up(*refs):
    total = refs[0][...].astype(F32)
    for ref in refs[1:-1]:
        total = total + ref[...].astype(F32)
    refs[-1][...] = total.astype(BF16)


def target_side(ws_ref, cot_ref, grad_ref, grad_received_ref, held_ref, held_received_ref, out_ref, updated_ref):
    core = here()[0]
    rows = cot_ref.shape[0]
    out_ref[...] = (
        cot_ref[...].astype(F32)
        + mm(grad_ref[0:rows, :], part(ws_ref, core), LANES)
        + mm(grad_received_ref[rows:, :], part(ws_ref, 1 - core), LANES)
    ).astype(BF16)
    half = held_ref.shape[1]
    updated_ref[:, pl.ds(pl.multiple_of(core * half, half), half)] = held_ref[...]
    updated_ref[:, pl.ds(pl.multiple_of((1 - core) * half, half), half)] = held_received_ref[...]


def project_back(total_ref, wm_ref, out_ref):
    out_ref[...] = mm(total_ref[...], wm_ref[...], LANES).astype(BF16)


def write_columns(quads, scales, side, refs, outs, buffer, sems, extra=()):
    core, quad, _, _ = here()
    count = quads // 2
    rows, half = refs[0].shape
    column = pl.multiple_of((core if side == 0 else 1 - core) * half, half)

    def copies(n):
        slot = quad ^ n
        row = pl.multiple_of((slot % count) * rows, rows)
        return slot // count, [
            pltpu.make_async_copy(buffer.at[n], out.at[pl.ds(row, rows), pl.ds(column, half)], sems.at[n]) for out in outs
        ]

    for copy in extra:
        copy.start()
    for n, ref in enumerate(refs):
        which, pair = copies(n)
        buffer[n] = ref[...].astype(F32) * jnp.where(which == 0, scales[0], scales[1])
        for k in range(2):
            pl.when(which == k)(pair[k].start)
    for n in range(quads):
        which, pair = copies(n)
        for k in range(2):
            pl.when(which == k)(pair[k].wait)
    for copy in extra:
        copy.wait()


def write_own(quads, scales, *refs):
    write_columns(quads, scales, 0, refs[:quads], refs[quads : quads + 2], *refs[quads + 2 :])


def finish(quads, scales, rows_ref, *refs):
    pieces, outs, (buffer, sems) = refs[:quads], refs[quads + 2 : quads + 5], refs[quads + 5 :]
    last = pltpu.make_async_copy(rows_ref, outs[2], sems.at[quads])
    write_columns(quads, scales, 1, pieces, outs[:2], buffer, sems, (last,))


def local(row_devices, blk_devices, source_table, target_table, message_weight, self_weight, tile_lists, key_offsets, list_lengths, cotangent):
    devices = row_devices * blk_devices
    targets, width = target_table.shape
    block_rows = source_table.shape[0]
    slots = tile_lists.shape[1]
    assert tile_lists.shape[0] == 1 and block_rows == targets and slots == blk_devices
    half = width // 2
    sides = blk_devices // 2
    quads = blk_devices
    layers = row_devices // 2
    share = block_rows // row_devices
    square = 2 * targets * width * width

    direct = list(range(2, blk_devices, 2))
    held = {m: swap(source_table, m, devices) for m in direct}

    blocks = lax.iota(jnp.int32, blk_devices)
    used = (tile_lists[0][None, :] == blocks[:, None]) & (lax.iota(jnp.int32, slots)[None, :] < list_lengths[0])
    links = jnp.max(jnp.where(used[:, :, None], key_offsets.T[None, :, :], -1), axis=1)
    links = jnp.concatenate([links, jnp.broadcast_to(list_lengths[:, None], (8 - slots % 8, targets))], axis=0)
    their_links = swap(links, 1, devices)

    table0, cot0 = target_table, cotangent
    held[1] = swap(source_table, 1, devices)
    table1 = swap(table0, 1, devices)
    cot1 = swap(cot0, 1, devices)

    columns, own0, gathered, weight = call(
        gather_first,
        "gather_first",
        (
            shaped((2 * targets, slots), jnp.int32),
            shaped((targets, half), F32),
            shaped((2 * targets, width), F32),
            shaped((width, half), BF16),
        ),
        inputs=5,
        moved=0,
        scratch_shapes=[pltpu.VMEM((slots, targets), jnp.int32)],
    )(links, their_links, source_table, table0, self_weight)
    ready = lax.optimization_barrier((columns, own0, gathered, weight, *[held[m] for m in direct]))
    columns, own0, gathered, weight = ready[:4]
    for m, value in zip(direct, ready[4:]):
        held[m] = value
        held[m + 1] = swap(value, 1, devices)
    order = [1, *direct]
    own1, gathered = call(
        functools.partial(gather_more, order),
        "gather_more",
        (shaped((targets, half), F32), shaped((2 * targets, width), F32)),
        inputs=4 + len(order),
        flops=2 * square,
    )(columns, gathered, table1, weight, *[held[m] for m in order])
    order = [m + 1 for m in direct]
    gathered, grad, updated, updated_there = call(
        functools.partial(forward, order),
        "forward",
        (shaped((2 * targets, width), BF16), shaped((2 * targets, half), BF16)) + (shaped((targets, half), BF16),) * 2,
        inputs=11 + len(order),
        flops=2 * sides * square,
    )(
        links, their_links, columns, gathered, own0, own1, message_weight, table0, table1, cot0, cot1,
        *[held[m] for m in order],
    )

    piece = 2 * width // quads
    terms = call(
        weight_terms,
        "weight_terms",
        [shaped((piece, half), F32)] + [shaped((piece, half), BF16)] * (quads - 1),
        inputs=4,
        flops=2 * square,
        scratch_shapes=[pltpu.VMEM((2 * width, half), F32)],
    )(table0, table1, gathered, grad)
    received = [swap(terms[m], 2 * m, devices) for m in reversed(range(1, quads))]

    terms, grad_sent, updated_there = lax.optimization_barrier((terms, grad, updated_there))
    grad_received = swap(grad_sent, 1, devices)
    updated_received = swap(updated_there, 1, devices)
    masks = [1 << i for i in range(quads.bit_length() - 1)]
    routes = (masks, masks[::-1])
    orders = [[sum(mask * ((j >> (len(masks) - 1 - i)) & 1) for i, mask in enumerate(route)) for j in range(quads)] for route in routes]
    half_rows = layers * share // 2
    count = quads // 2 * half_rows
    terms, grad_received = lax.optimization_barrier((terms, grad_received))
    sources = call(
        functools.partial(source_terms, share, sides, orders),
        "source_terms",
        [shaped((count, width), F32), shaped((count, width), BF16)] * 2,
        inputs=4,
        flops=4 * square,
    )(links, their_links, grad, grad_received)
    target_gradient, updated = call(
        target_side, "target_side", (shaped((targets, width), BF16),) * 2, inputs=6
    )(self_weight, cot0, grad, grad_received, updated, updated_received)
    _, received, target_gradient, updated = lax.optimization_barrier((sources, received, target_gradient, updated))

    state = [[sources[0], sources[1]], [sources[2], sources[3]]]

    def source_step(n):
        return [swap(state[k][1], 2 * routes[k][n], devices) for k in range(2)]

    def source_add(n, came):
        for k in range(2):
            if n == len(masks) - 1:
                outs = [shaped((half_rows, width), (F32, BF16)[k])]
            else:
                rows = state[k][0].shape[0] // 2
                outs = [shaped((rows, width), F32), shaped((rows, width), BF16)]
            state[k] = call(halve, "source_sum", outs, inputs=2)(state[k][0], came[k])

    total = call(add_up, "weight_sum", shaped((piece, half), BF16), inputs=quads)(terms[0], *received)
    mask, n = 1, 0
    while mask < layers:
        other = swap(total, 2 * quads * mask, devices)
        came = source_step(n)
        total = call(add_up, "weight_sum", shaped((piece, half), BF16), inputs=2)(total, other)
        source_add(n, came)
        mask, n = 2 * mask, n + 1
    while n < len(masks):
        source_add(n, source_step(n))
        n += 1
    stays, goes = state[0][0], state[1][0]
    total = lax.optimization_barrier((total, goes))[0]
    pieces = {0: total}
    for m in reversed(range(1, quads)):
        pieces[m] = swap(total, 2 * m, devices)

    mask = 1
    while mask < layers:
        came = swap(goes, 2 * quads * mask, devices)
        mask *= 2
        if mask == layers:
            rounded = call(halve, "source_sum", [shaped((share, width), BF16)], inputs=2)(stays, came)[0]
            source_rows = call(project_back, "project_back", pltpu.VMEM((share, width), BF16), inputs=2)(
                swap(rounded, 1, devices), message_weight
            )
        else:
            rows = stays.shape[0] // 2
            stays, goes = call(halve, "source_sum", [shaped((rows, width), F32), shaped((rows, width), BF16)], inputs=2)(
                stays, came
            )

    their_pieces = {m: swap(value, 1, devices) for m, value in pieces.items()}
    scales = ((targets * devices) ** (-0.5), (block_rows * blk_devices) ** (-0.5))
    written = call(
        functools.partial(write_own, quads, scales),
        "write_own",
        (shaped((width, width), F32),) * 2,
        inputs=quads,
        out_specs=(HBM, HBM),
        scratch_shapes=[pltpu.VMEM((quads, piece, half), F32), pltpu.SemaphoreType.DMA((quads,))],
    )(*[pieces[m] for m in range(quads)])
    self_gradient, message_gradient, source_gradient = call(
        functools.partial(finish, quads, scales),
        "finish",
        (shaped((width, width), F32),) * 2 + (shaped((share, width), BF16),),
        in_specs=[VMEM] * (1 + quads) + [HBM] * 2,
        out_specs=(HBM, HBM, HBM),
        input_output_aliases={1 + quads: 0, 2 + quads: 1},
        scratch_shapes=[pltpu.VMEM((quads, piece, half), F32), pltpu.SemaphoreType.DMA((quads + 1,))],
    )(source_rows, *[their_pieces[m] for m in range(quads)], *written)
    return (updated, target_gradient, source_gradient, self_gradient, message_gradient)


def solution(mesh):
    split = P(AXES, None)
    return jax.shard_map(
        functools.partial(local, mesh.shape["row"], mesh.shape["blk"]),
        mesh=mesh,
        in_specs=(P("blk", None), split, P(), P(), split, split, P(AXES), split),
        out_specs=(split, split, P(("blk", "row"), None), P(), P()),
        check_vma=False,
    )
```
